128 devices in a mesh: seq: 16 (over z, y), chan: 8 (over x, core).
Axes of the slice: x: 4, y: 4, z: 4, core: 2. Of those that a mesh axis runs over, the one named last changes fastest.
Arguments:
- inputs: bfloat16 [8192, 4096], P('seq', 'chan'), may hold values from -6 to 6
- out_grad: bfloat16 [8192, 4096], P('seq', 'chan'), may hold values from -0.0034179688 to 0.0034179688
- embed_weight: float32 [17, 64], replicated, may hold values from -1.5 to 1.5
- embed_bias: float32 [64], replicated, may hold values from -1 to 1
- embed_freq: float32 [64], replicated, may hold values from 0.5 to 2
- mixer_weight: float32 [64, 64], replicated, may hold values from -0.75 to 0.75
- mixer_bias: float32 [64], replicated, may hold values from -1 to 1
- mixer_freq: float32 [64], replicated, may hold values from 0.5 to 2
- head_weight: float32 [64, 4096], P(None, 'chan'), may hold values from -0.75 to 0.75
- decay_rates: float32 [4096], P('chan'), may hold values from 1 to 12
Outputs:
- embed_weight_grad: float32 [17, 64], replicated
- embed_bias_grad: float32 [64], replicated
- embed_freq_grad: float32 [64], replicated
- mixer_weight_grad: float32 [64, 64], replicated
- mixer_bias_grad: float32 [64], replicated
- mixer_freq_grad: float32 [64], replicated
- head_weight_grad: float32 [64, 4096], P(None, 'chan')
- decay_rates_grad: float32 [4096], P('chan')
The draws below stay inside these ranges and needn't reach their ends.
All inputs are finite; a program needn't handle non-finite values.
Results may differ from the reference program's by a relative error of at most 0.0003.
Values may be sent and summed in bfloat16 or wider, within the bound.
A program may use at most 128 MiB of HBM per device.

```python
import math
import jax
import jax.numpy as jnp
from jax import lax

CHANNELS = 4096
NET_HIDDEN = 64
BANDS = 8
FEATURES = 17
FILTER_LEN = 1536
TOKENS = 8192


def levels(rng, dims, shards, least, top_value):
    def one(dim, shards_of):
        steps = jax.random.uniform(jax.random.fold_in(jax.random.fold_in(rng, 6), dim), (shards_of,), jnp.float32, least / len(shards), top_value / len(shards))
        return jnp.repeat(jnp.exp(steps), dims[dim] // shards_of).reshape((-1,) + (1,) * (len(dims) - dim - 1))

    factor_of = one(*shards[0])
    for cut in shards[1:]:
        factor_of = factor_of * one(*cut)
    return factor_of


def noise(own_key, shape, width, most, shards=(), kind=jnp.bfloat16):
    result = width * jax.random.normal(own_key, shape, jnp.float32)
    if shards:
        result = result * levels(own_key, shape, shards, -0.22, 0.18)
    return jnp.clip(result, -most, most).astype(kind)


def setup_inputs(seed: int = 0) -> dict:
    seeds = jax.random.split(jax.random.key(seed), 11)
    inputs = noise(seeds[0], (TOKENS, CHANNELS), 1.0, 6.0, ((0, 16), (1, 8)))
    out_grad = noise(seeds[1], (TOKENS, CHANNELS), (2.0 / (TOKENS * FILTER_LEN) ** 0.5), 0.0034179688, ((0, 16), (1, 8)))
    embed_weight = noise(seeds[2], (FEATURES, NET_HIDDEN), FEATURES ** -0.5, 1.5, (), jnp.float32)
    embed_bias = jnp.clip(jax.random.uniform(seeds[3], (NET_HIDDEN,), jnp.float32, -1.0, 1.0), -1.0, 1.0)
    embed_freq = jnp.clip(jnp.exp(jax.random.uniform(seeds[4], (NET_HIDDEN,), jnp.float32, math.log(0.5), math.log(2.0))), 0.5, 2.0)
    mixer_weight = noise(seeds[5], (NET_HIDDEN, NET_HIDDEN), NET_HIDDEN ** -0.5, 0.75, (), jnp.float32)
    mixer_bias = jnp.clip(jax.random.uniform(seeds[6], (NET_HIDDEN,), jnp.float32, -1.0, 1.0), -1.0, 1.0)
    mixer_freq = jnp.clip(jnp.exp(jax.random.uniform(seeds[7], (NET_HIDDEN,), jnp.float32, math.log(0.5), math.log(2.0))), 0.5, 2.0)
    head_weight = noise(seeds[8], (NET_HIDDEN, CHANNELS), NET_HIDDEN ** -0.5, 0.75, ((1, 8),), jnp.float32)
    decay_rates = jnp.clip(jnp.exp(math.log(12.0) - 2.4849066 * jax.random.uniform(seeds[9], (CHANNELS,), jnp.float32) ** levels(seeds[9], (CHANNELS,), ((0, 8),), -0.2, 0.2)), 1.0, 12.0)
    return {"inputs": inputs, "out_grad": out_grad, "embed_weight": embed_weight, "embed_bias": embed_bias, "embed_freq": embed_freq, "mixer_weight": mixer_weight, "mixer_bias": mixer_bias, "mixer_freq": mixer_freq, "head_weight": head_weight, "decay_rates": decay_rates}


EXACT = lax.Precision.HIGHEST

def tap_features(tap_index, filter_len, band_count):
    scaled = tap_index.astype(jnp.float32) / filter_len
    band_freqs = jnp.array([max(1, filter_len // 4 // 2 ** (band_count - band_level)) for band_level in range(1, band_count + 1)], dtype=jnp.int32)
    cycles = band_freqs[:, None] * tap_index[None, :] % filter_len
    band_angle = cycles.astype(jnp.float32) * (2.0 * math.pi / filter_len)
    return (scaled, jnp.concatenate([scaled[None, :], jnp.cos(band_angle), jnp.sin(band_angle)], axis=0))

def filter_values(embed_weight, embed_bias, embed_freq, mixer_weight, mixer_bias, mixer_freq, head_weight, decay_rates):
    tap_index = jnp.arange(FILTER_LEN, dtype=jnp.int32)
    scaled, features = tap_features(tap_index, FILTER_LEN, BANDS)
    first_pre = jnp.dot(embed_weight.T, features, precision=EXACT, preferred_element_type=jnp.float32) + embed_bias[:, None]
    first_act = jnp.sin(embed_freq[:, None] * first_pre)
    second_pre = jnp.dot(mixer_weight.T, first_act, precision=EXACT, preferred_element_type=jnp.float32) + mixer_bias[:, None]
    second_act = jnp.sin(mixer_freq[:, None] * second_pre)
    shaped = jnp.dot(second_act.T, head_weight, precision=EXACT, preferred_element_type=jnp.float32)
    return shaped * jnp.exp(-scaled[:, None] * decay_rates[None, :])

def correlate_group(pair):
    group_in, group_grad = pair
    fft_length = 2 * TOKENS
    in_spec = jnp.fft.rfft(group_in, n=fft_length, axis=0)
    grad_spec = jnp.fft.rfft(group_grad, n=fft_length, axis=0)
    return jnp.fft.irfft(jnp.conj(in_spec) * grad_spec, n=fft_length, axis=0)[:FILTER_LEN]

def reference(inputs, out_grad, embed_weight, embed_bias, embed_freq, mixer_weight, mixer_bias, mixer_freq, head_weight, decay_rates):
    group_size = 128
    group_count = CHANNELS // group_size
    in_groups = inputs.astype(jnp.float32).reshape(TOKENS, group_count, group_size).transpose(1, 0, 2)
    grad_groups = out_grad.astype(jnp.float32).reshape(TOKENS, group_count, group_size).transpose(1, 0, 2)
    filter_grad = lax.map(correlate_group, (in_groups, grad_groups))
    filter_grad = filter_grad.transpose(1, 0, 2).reshape(FILTER_LEN, CHANNELS)
    filter_now, pullback = jax.vjp(filter_values, embed_weight, embed_bias, embed_freq, mixer_weight, mixer_bias, mixer_freq, head_weight, decay_rates)
    grad_ew, grad_eb, grad_ef, grad_mw, grad_mb, grad_mf, grad_hw, grad_dr = pullback(filter_grad)
    return (grad_ew, grad_eb, grad_ef, grad_mw, grad_mb, grad_mf, grad_hw, grad_dr)
```

```python
import math

import jax
import jax.numpy as jnp
import numpy as np
from jax import lax
from jax.experimental import pallas as pl
from jax.experimental.pallas import tpu as pltpu
from jax.sharding import PartitionSpec as P

MESH = pl.DeviceIdType.MESH
EXACT = lax.Precision.HIGHEST
F32 = jnp.float32
BF16 = jnp.bfloat16

FILTER_LEN = 1536
BANDS = 8
FEATURES = 17
FEATURE_ROWS = 24
HIDDEN = 64
BLOCK = 512
SEQ = 16
CHAN = 8
OWN = 32
PARTS = 3
SEQ_SIDE = 4


def transform_table():
    order = np.concatenate([np.arange(0, BLOCK, 2), np.arange(1, BLOCK, 2)])
    turns = (2 * order[None, :] + 1) * np.arange(BLOCK)[:, None] % (4 * BLOCK)
    angle = turns * (2.0 * math.pi / (4 * BLOCK))
    table = np.concatenate([np.cos(angle), -np.sin(angle)], axis=1)
    high = table.astype(BF16)
    low = (table - high.astype(np.float64)).astype(BF16)
    return high, low


def tap_table():
    taps = np.arange(FILTER_LEN)
    freqs = np.array([max(1, FILTER_LEN // 4 // 2 ** (BANDS - level)) for level in range(1, BANDS + 1)])
    angle = (freqs[:, None] * taps[None, :] % FILTER_LEN) * (2.0 * math.pi / FILTER_LEN)
    table = np.zeros((FEATURE_ROWS, FILTER_LEN), np.float32)
    table[0] = taps / FILTER_LEN
    table[1 : 1 + BANDS] = np.cos(angle)
    table[1 + BANDS : FEATURES] = np.sin(angle)
    table[FEATURES] = 1.0
    return table


def dot(a, b, a_dim=1, b_dim=0, precision=EXACT):
    return lax.dot_general(
        a, b, (((a_dim,), (b_dim,)), ((), ())), precision=precision, preferred_element_type=F32
    )


def sin_cos(a):
    turns = jnp.floor(a * (2.0 / math.pi) + 0.5)
    r = a - turns * 1.5703125
    r = r - turns * 4.837512969970703125e-4
    r = r - turns * 7.549789954891882e-8
    r2 = r * r
    s = r + r * r2 * (-1.6666654611e-1 + r2 * (8.3321608736e-3 + r2 * -1.9515295891e-4))
    c = 1.0 - 0.5 * r2 + r2 * r2 * (4.166664568298827e-2 + r2 * (-1.388731625493765e-3 + r2 * 2.443315711809948e-5))
    q = turns.astype(jnp.int32)
    odd = (q & 1) == 1
    sine = jnp.where(odd, c, s)
    cosine = jnp.where(odd, s, c)
    sine = jnp.where((q & 2) == 2, -sine, sine)
    cosine = jnp.where(((q + 1) & 2) == 2, -cosine, cosine)
    return sine, cosine


def column(row):
    n = row.shape[1]
    hit = lax.broadcasted_iota(jnp.int32, (n, n), 0) == lax.broadcasted_iota(jnp.int32, (n, n), 1)
    return jnp.sum(jnp.where(hit, row, 0.0), axis=1, keepdims=True)


def kernel(
    x_hbm, g_hbm, ew, eb, ef, mw, mb, mf, hw, dr, high_hbm, low_hbm, feat,
    ew_out, eb_out, ef_out, mw_out, mb_out, mf_out, hw_out, dr_out,
    x_in, g_in, high, low, send, recv, spec, prod, lags,
    first_pre, first_cos, first_act, second_pre, second_cos, second_act, shaped, envelope,
    head_all, part, sum_recv, tile, tile_recv, total,
    local_sem, a2a_send, a2a_recv, head_send, head_recv, sum_send, sum_got, tile_send, tile_got, all_send, all_got,
):
    s = lax.axis_index("seq")
    c = lax.axis_index("chan")
    z = s // SEQ_SIDE
    y = s % SEQ_SIDE

    loads = [
        pltpu.make_async_copy(src, dst, local_sem.at[i])
        for i, (src, dst) in enumerate([(x_hbm, x_in), (g_hbm, g_in), (high_hbm, high), (low_hbm, low)])
    ]
    for load in loads:
        load.start()

    barrier = pltpu.get_barrier_semaphore()
    for d in range(1, SEQ):
        pl.semaphore_signal(barrier, inc=1, device_id=((s + d) % SEQ, c), device_id_type=MESH)
    for d in range(1, CHAN):
        pl.semaphore_signal(barrier, inc=1, device_id=(s, (c + d) % CHAN), device_id_type=MESH)

    loads[0].wait()
    loads[1].wait()

    def a2a(slot, peer):
        return pltpu.make_async_remote_copy(
            src_ref=send.at[peer], dst_ref=recv.at[slot], send_sem=a2a_send.at[peer], recv_sem=a2a_recv.at[slot],
            device_id=(peer, c), device_id_type=MESH,
        )

    for t in range(SEQ_SIDE):
        plane = (z + (2, 1, 3, 0)[t]) % SEQ_SIDE
        lanes = pl.ds(pl.multiple_of(plane * 128, 128), 128)
        send[pl.ds(plane * SEQ_SIDE, SEQ_SIDE), 0:OWN, :] = x_in[:, lanes].T.reshape(SEQ_SIDE, OWN, BLOCK)
        send[pl.ds(plane * SEQ_SIDE, SEQ_SIDE), OWN : 2 * OWN, :] = g_in[:, lanes].T.reshape(SEQ_SIDE, OWN, BLOCK)
        if t == 0:
            pl.semaphore_wait(barrier, SEQ + CHAN - 2)
        for k in range(SEQ_SIDE if t < 3 else SEQ_SIDE - 1):
            peer = plane * SEQ_SIDE + (y + (2, 1, 3, 0)[k]) % SEQ_SIDE
            a2a(s, peer).start()
    recv[s] = send[s]

    ef_col = column(ef[...])
    mf_col = column(mf[...])
    features = feat[...]
    pre = dot(ew[...], features[:FEATURES, :], 0, 0) + column(eb[...])
    first_pre[...] = pre
    act, slope = sin_cos(ef_col * pre)
    first_act[...] = act
    first_cos[...] = slope
    pre = dot(mw[...], act, 0, 0) + column(mb[...])
    second_pre[...] = pre
    act, slope = sin_cos(mf_col * pre)
    second_act[...] = act
    second_cos[...] = slope
    pick = lax.broadcasted_iota(jnp.int32, (OWN, BLOCK), 1) == lax.broadcasted_iota(jnp.int32, (OWN, BLOCK), 0) + OWN * s
    rates = jnp.sum(jnp.where(pick, dr[...], 0.0), axis=1, keepdims=True)
    picked = jnp.where(pick, 1.0, 0.0).astype(F32)
    head_rows = dot(picked, hw[...], 1, 1)
    head_cols = dot(hw[...], picked, 1, 1)
    shaped[...] = dot(head_rows, act)
    envelope[...] = jnp.exp(-features[0:1, :] * rates)

    loads[2].wait()
    loads[3].wait()
    for t in range(SEQ_SIDE):
        plane = (z + (0, 3, 1, 2)[t]) % SEQ_SIDE
        for k in range(SEQ_SIDE if t > 0 else SEQ_SIDE - 1):
            peer = plane * SEQ_SIDE + (y + (3, 1, 2, 0)[k]) % SEQ_SIDE
            a2a(peer, peer).wait_recv()
        blocks = recv[pl.ds(plane * SEQ_SIDE, SEQ_SIDE)].reshape(SEQ_SIDE * 2 * OWN, BLOCK)

        def transform(j, _):
            lanes = pl.ds(pl.multiple_of(j * 256, 256), 256)
            got = jnp.dot(blocks, high[:, lanes], preferred_element_type=F32)
            got += jnp.dot(blocks, low[:, lanes], preferred_element_type=F32)
            spec[pl.ds(plane * SEQ_SIDE, SEQ_SIDE), :, lanes] = got.reshape(SEQ_SIDE, 2 * OWN, 256)
            return 0

        lax.fori_loop(0, 4, transform, 0)

    def multiply(i, _):
        row = pl.multiple_of(i // 4 * 8, 8)
        lane = pl.multiple_of(i % 4 * 128, 128)
        sign = jnp.where(i % 4 < 2, 1.0, -1.0).astype(F32)
        re, im = pl.ds(lane, 128), pl.ds(lane + BLOCK, 128)
        xs, total_re, total_im = [], [None] * 4, [None] * 4
        for b in range(SEQ):
            xs.append((spec[b, pl.ds(row, 8), re], spec[b, pl.ds(row, 8), im]))
            g_re, g_im = spec[b, pl.ds(row + OWN, 8), re], spec[b, pl.ds(row + OWN, 8), im]
            for m in range(min(b, PARTS) + 1):
                x_re, x_im = xs[b - m]
                add_re = x_re * g_re + x_im * g_im
                add_im = x_re * g_im - x_im * g_re
                total_re[m] = add_re if total_re[m] is None else total_re[m] + add_re
                total_im[m] = add_im if total_im[m] is None else total_im[m] + add_im
        for p in range(PARTS):
            prod[pl.ds(p * OWN + row, 8), re] = total_re[p] + sign * total_im[p + 1]
            prod[pl.ds(p * OWN + row, 8), im] = total_im[p] - sign * total_re[p + 1]
        return 0

    lax.fori_loop(0, 16, multiply, 0)

    weights = prod[...] * (1.0 / BLOCK)
    weights_high = weights.astype(BF16)
    weights_low = (weights - weights_high.astype(F32)).astype(BF16)

    def invert(j, _):
        rows = pl.ds(pl.multiple_of(j * 256, 256), 256)
        got = dot(weights_high, high[rows, :], 1, 1, None)
        got += dot(weights_low, high[rows, :], 1, 1, None)
        got += dot(weights_high, low[rows, :], 1, 1, None)
        for p in range(PARTS):
            lags[:, pl.ds(pl.multiple_of(p * BLOCK + j * 256, 256), 256)] = got[p * OWN : (p + 1) * OWN, :]
        return 0

    lax.fori_loop(0, 2, invert, 0)

    out_delta = lags[...] * envelope[...]
    mine = pl.ds(pl.multiple_of(s * OWN, OWN), OWN)
    head_all[mine, 0:HIDDEN] = dot(out_delta, second_act[...], 1, 1)
    rate_grad = -jnp.sum(out_delta * shaped[...] * feat[0:1, :], axis=1, keepdims=True)
    head_all[mine, HIDDEN:128] = jnp.broadcast_to(rate_grad, (OWN, 128 - HIDDEN))

    def head_copy(slot, peer):
        rows = pl.ds(pl.multiple_of(slot * OWN, OWN), OWN)
        return pltpu.make_async_remote_copy(
            src_ref=head_all.at[rows], dst_ref=head_all.at[rows], send_sem=head_send.at[peer], recv_sem=head_recv.at[slot],
            device_id=(peer, c), device_id_type=MESH,
        )

    for d in range(1, SEQ):
        head_copy(s, (s + d) % SEQ).start()

    second_grad = dot(head_cols, out_delta)
    second_slope = second_grad * second_cos[...]
    second_delta = second_slope * mf_col
    ones = feat[FEATURES : FEATURES + 1, :]
    part[:, 0:HIDDEN] = dot(first_act[...], second_delta, 1, 1)
    first_grad = dot(mw[...], second_delta)
    first_slope = first_grad * first_cos[...]
    first_delta = first_slope * ef_col
    part[0:FEATURE_ROWS, HIDDEN:128] = dot(features, first_delta, 1, 1)
    ones = jnp.broadcast_to(ones, (8, FILTER_LEN))
    part[24:32, HIDDEN:128] = dot(ones, first_slope * first_pre[...], 1, 1)
    part[32:40, HIDDEN:128] = dot(ones, second_delta, 1, 1)
    part[40:48, HIDDEN:128] = dot(ones, second_slope * second_pre[...], 1, 1)
    part[48:64, HIDDEN:128] = jnp.zeros((16, 128 - HIDDEN), F32)

    def sum_copy(slot, peer):
        return pltpu.make_async_remote_copy(
            src_ref=part.at[pl.ds(pl.multiple_of(peer * 8, 8), 8)], dst_ref=sum_recv.at[slot],
            send_sem=sum_send.at[peer], recv_sem=sum_got.at[slot], device_id=(s, peer), device_id_type=MESH,
        )

    for d in range(1, CHAN):
        sum_copy(c, (c + d) % CHAN).start()
    sum_recv[c] = part[pl.ds(pl.multiple_of(c * 8, 8), 8), :]
    for d in range(1, CHAN):
        peer = (c + d) % CHAN
        sum_copy(peer, peer).wait_recv()
    tile[...] = jnp.sum(sum_recv[...], axis=0)

    def tile_copy(slot, peer):
        return pltpu.make_async_remote_copy(
            src_ref=tile, dst_ref=tile_recv.at[slot], send_sem=tile_send.at[peer], recv_sem=tile_got.at[slot],
            device_id=(peer, c), device_id_type=MESH,
        )

    for d in range(1, SEQ):
        tile_copy(s, (s + d) % SEQ).start()
    tile_recv[s] = tile[...]
    for d in range(1, SEQ):
        peer = (s + d) % SEQ
        tile_copy(peer, peer).wait_recv()
    total[c] = jnp.sum(tile_recv[...], axis=0)

    def all_copy(slot, peer):
        return pltpu.make_async_remote_copy(
            src_ref=total.at[slot], dst_ref=total.at[slot], send_sem=all_send.at[peer], recv_sem=all_got.at[slot],
            device_id=(s, peer), device_id_type=MESH,
        )

    for d in range(1, CHAN):
        all_copy(c, (c + d) % CHAN).start()

    for d in range(1, SEQ):
        peer = (s + d) % SEQ
        head_copy(peer, peer).wait_recv()
    turned = head_all[...].T
    hw_out[...] = turned[0:HIDDEN, :]
    dr_out[...] = turned[HIDDEN : HIDDEN + 1, :]

    for d in range(1, CHAN):
        peer = (c + d) % CHAN
        all_copy(peer, peer).wait_recv()
    done = total[...].reshape(HIDDEN, 128)
    mw_out[...] = done[:, 0:HIDDEN]
    ew_out[...] = done[0:FEATURES, HIDDEN:128]
    eb_out[...] = done[FEATURES : FEATURES + 1, HIDDEN:128]
    ef_out[...] = done[24:25, HIDDEN:128]
    mb_out[...] = done[32:33, HIDDEN:128]
    mf_out[...] = done[40:41, HIDDEN:128]

    for d in range(1, SEQ):
        peer = (s + d) % SEQ
        a2a(s, peer).wait_send()
        head_copy(s, peer).wait_send()
        tile_copy(s, peer).wait_send()
    for d in range(1, CHAN):
        peer = (c + d) % CHAN
        sum_copy(c, peer).wait_send()
        all_copy(c, peer).wait_send()


def shards(inputs, out_grad, ew, eb, ef, mw, mb, mf, hw, dr):
    high, low = transform_table()
    row = lambda v: v.reshape(1, -1)
    vmem = pl.BlockSpec(memory_space=pltpu.VMEM)
    anywhere = pl.BlockSpec(memory_space=pl.ANY)
    out = lambda *shape: jax.ShapeDtypeStruct(shape, F32)
    taps = lambda rows: pltpu.VMEM((rows, FILTER_LEN), F32)
    dma = lambda n: pltpu.SemaphoreType.DMA((n,))
    got = pl.pallas_call(
        kernel,
        out_shape=(
            out(FEATURES, HIDDEN), out(1, HIDDEN), out(1, HIDDEN), out(HIDDEN, HIDDEN), out(1, HIDDEN), out(1, HIDDEN),
            out(HIDDEN, BLOCK), out(1, BLOCK),
        ),
        in_specs=[anywhere] * 2 + [vmem] * 8 + [anywhere] * 2 + [vmem],
        out_specs=(vmem,) * 8,
        scratch_shapes=[
            pltpu.VMEM((BLOCK, BLOCK), BF16), pltpu.VMEM((BLOCK, BLOCK), BF16),
            pltpu.VMEM((BLOCK, 2 * BLOCK), BF16), pltpu.VMEM((BLOCK, 2 * BLOCK), BF16),
            pltpu.VMEM((SEQ, 2 * OWN, BLOCK), BF16), pltpu.VMEM((SEQ, 2 * OWN, BLOCK), BF16),
            pltpu.VMEM((SEQ, 2 * OWN, 2 * BLOCK), F32), pltpu.VMEM((PARTS * OWN, 2 * BLOCK), F32),
            taps(OWN),
            taps(HIDDEN), taps(HIDDEN), taps(HIDDEN), taps(HIDDEN), taps(HIDDEN), taps(HIDDEN), taps(OWN), taps(OWN),
            pltpu.VMEM((BLOCK, 128), F32), pltpu.VMEM((HIDDEN, 128), F32), pltpu.VMEM((CHAN, 8, 128), F32),
            pltpu.VMEM((8, 128), F32), pltpu.VMEM((SEQ, 8, 128), F32), pltpu.VMEM((CHAN, 8, 128), F32),
            dma(4), dma(SEQ), dma(SEQ), dma(SEQ), dma(SEQ), dma(CHAN), dma(CHAN), dma(SEQ), dma(SEQ), dma(CHAN), dma(CHAN),
        ],
        compiler_params=pltpu.CompilerParams(
            collective_id=0, has_side_effects=True, vmem_limit_bytes=40 * 1024 * 1024
        ),
    )(
        inputs, out_grad, ew, row(eb), row(ef), mw, row(mb), row(mf), hw, row(dr),
        jnp.asarray(high), jnp.asarray(low), jnp.asarray(tap_table()),
    )
    ew_g, eb_g, ef_g, mw_g, mb_g, mf_g, hw_g, dr_g = got
    flat = lambda v: v.reshape(-1)
    return ew_g, flat(eb_g), flat(ef_g), mw_g, flat(mb_g), flat(mf_g), hw_g, flat(dr_g)


def solution(mesh):
    return jax.shard_map(
        shards,
        mesh=mesh,
        in_specs=(
            P("seq", "chan"), P("seq", "chan"), P(), P(), P(), P(), P(), P(), P(None, "chan"), P("chan"),
        ),
        out_specs=(P(), P(), P(), P(), P(), P(), P(None, "chan"), P("chan")),
        check_vma=False,
    )
```

```python
import math

import jax
import jax.numpy as jnp
import numpy as np
from jax import lax
from jax.experimental import pallas as pl
from jax.experimental.pallas import tpu as pltpu
from jax.sharding import PartitionSpec as P

MESH = pl.DeviceIdType.MESH
EXACT = lax.Precision.HIGHEST
F32 = jnp.float32
BF16 = jnp.bfloat16

FILTER_LEN = 1536
BANDS = 8
FEATURES = 17
FEATURE_ROWS = 24
HIDDEN = 64
BLOCK = 512
SEQ = 16
CHAN = 8
OWN = 32
PARTS = 3
SEQ_SIDE = 4
VMEM_LIMIT = 60 * 1024 * 1024


def transform_table():
    order = np.concatenate([np.arange(0, BLOCK, 2), np.arange(1, BLOCK, 2)])
    turns = (2 * order[None, :] + 1) * np.arange(BLOCK)[:, None] % (4 * BLOCK)
    angle = turns * (2.0 * math.pi / (4 * BLOCK))
    table = np.concatenate([np.cos(angle), -np.sin(angle)], axis=1)
    high = table.astype(BF16)
    low = (table - high.astype(np.float64)).astype(BF16)
    return high, low


def tap_table():
    taps = np.arange(FILTER_LEN)
    freqs = np.array([max(1, FILTER_LEN // 4 // 2 ** (BANDS - level)) for level in range(1, BANDS + 1)])
    angle = (freqs[:, None] * taps[None, :] % FILTER_LEN) * (2.0 * math.pi / FILTER_LEN)
    table = np.zeros((FEATURE_ROWS, FILTER_LEN), np.float32)
    table[0] = taps / FILTER_LEN
    table[1 : 1 + BANDS] = np.cos(angle)
    table[1 + BANDS : FEATURES] = np.sin(angle)
    table[FEATURES] = 1.0
    return table


def dot(a, b, a_dim=1, b_dim=0, precision=EXACT):
    return lax.dot_general(
        a, b, (((a_dim,), (b_dim,)), ((), ())), precision=precision, preferred_element_type=F32
    )


def sin_cos(a):
    turns = jnp.floor(a * (2.0 / math.pi) + 0.5)
    r = a - turns * 1.5703125
    r = r - turns * 4.837512969970703125e-4
    r = r - turns * 7.549789954891882e-8
    r2 = r * r
    s = r + r * r2 * (-1.6666654611e-1 + r2 * (8.3321608736e-3 + r2 * -1.9515295891e-4))
    c = 1.0 - 0.5 * r2 + r2 * r2 * (4.166664568298827e-2 + r2 * (-1.388731625493765e-3 + r2 * 2.443315711809948e-5))
    q = turns.astype(jnp.int32)
    odd = (q & 1) == 1
    sine = jnp.where(odd, c, s)
    cosine = jnp.where(odd, s, c)
    sine = jnp.where((q & 2) == 2, -sine, sine)
    cosine = jnp.where(((q + 1) & 2) == 2, -cosine, cosine)
    return sine, cosine


def column(row):
    n = row.shape[1]
    hit = lax.broadcasted_iota(jnp.int32, (n, n), 0) == lax.broadcasted_iota(jnp.int32, (n, n), 1)
    return jnp.sum(jnp.where(hit, row, 0.0), axis=1, keepdims=True)


def kernel(
    x_hbm, g_hbm, high_hbm, low_hbm, feat_hbm, ew_hbm, eb_hbm, ef_hbm, mw_hbm, mb_hbm, mf_hbm, hw_hbm, dr_hbm,
    ew_out, eb_out, ef_out, mw_out, mb_out, mf_out, hw_out, dr_out,
    x_in, g_in, high, low, feat, ew, eb, ef, mw, mb, mf, hw, dr, send, recv, spec, prod, lags,
    first_pre, first_cos, first_act, second_pre, second_cos, second_act, shaped, envelope,
    head_all, part, sum_recv, tile, tile_recv, total,
    local_sem, a2a_send, a2a_recv, head_send, head_recv, sum_send, sum_got, tile_send, tile_got, all_send, all_got,
):
    s = lax.axis_index("seq")
    c = lax.axis_index("chan")
    z = s // SEQ_SIDE
    y = s % SEQ_SIDE

    loads = [
        pltpu.make_async_copy(src, dst, local_sem.at[i])
        for i, (src, dst) in enumerate([
            (x_hbm, x_in), (g_hbm, g_in), (feat_hbm, feat), (ew_hbm, ew), (eb_hbm, eb), (ef_hbm, ef), (mw_hbm, mw),
            (mb_hbm, mb), (mf_hbm, mf), (hw_hbm, hw), (dr_hbm, dr), (high_hbm, high), (low_hbm, low),
        ])
    ]
    for load in loads:
        load.start()

    barrier = pltpu.get_barrier_semaphore()
    for d in range(1, SEQ):
        pl.semaphore_signal(barrier, inc=1, device_id=((s + d) % SEQ, c), device_id_type=MESH)
    for d in range(1, CHAN):
        pl.semaphore_signal(barrier, inc=1, device_id=(s, (c + d) % CHAN), device_id_type=MESH)

    loads[0].wait()
    loads[1].wait()

    def a2a(slot, peer):
        return pltpu.make_async_remote_copy(
            src_ref=send.at[peer], dst_ref=recv.at[slot], send_sem=a2a_send.at[peer], recv_sem=a2a_recv.at[slot],
            device_id=(peer, c), device_id_type=MESH,
        )

    for t in range(SEQ_SIDE):
        plane = (z + (2, 1, 3, 0)[t]) % SEQ_SIDE
        lanes = pl.ds(pl.multiple_of(plane * 128, 128), 128)
        send[pl.ds(plane * SEQ_SIDE, SEQ_SIDE), 0:OWN, :] = x_in[:, lanes].T.reshape(SEQ_SIDE, OWN, BLOCK)
        send[pl.ds(plane * SEQ_SIDE, SEQ_SIDE), OWN : 2 * OWN, :] = g_in[:, lanes].T.reshape(SEQ_SIDE, OWN, BLOCK)
        if t == 0:
            pl.semaphore_wait(barrier, SEQ + CHAN - 2)
        for k in range(SEQ_SIDE if t < 3 else SEQ_SIDE - 1):
            peer = plane * SEQ_SIDE + (y + (2, 1, 3, 0)[k]) % SEQ_SIDE
            a2a(s, peer).start()
    recv[s] = send[s]

    for load in loads[2:11]:
        load.wait()
    ef_col = column(ef[...])
    mf_col = column(mf[...])
    features = feat[...]
    pre = dot(ew[...], features[:FEATURES, :], 0, 0) + column(eb[...])
    first_pre[...] = pre
    act, slope = sin_cos(ef_col * pre)
    first_act[...] = act
    first_cos[...] = slope
    pre = dot(mw[...], act, 0, 0) + column(mb[...])
    second_pre[...] = pre
    act, slope = sin_cos(mf_col * pre)
    second_act[...] = act
    second_cos[...] = slope
    pick = lax.broadcasted_iota(jnp.int32, (OWN, BLOCK), 1) == lax.broadcasted_iota(jnp.int32, (OWN, BLOCK), 0) + OWN * s
    rates = jnp.sum(jnp.where(pick, dr[...], 0.0), axis=1, keepdims=True)
    picked = jnp.where(pick, 1.0, 0.0).astype(F32)
    head_rows = dot(picked, hw[...], 1, 1)
    head_cols = dot(hw[...], picked, 1, 1)
    shaped[...] = dot(head_rows, act)
    envelope[...] = jnp.exp(-features[0:1, :] * rates)

    loads[11].wait()
    loads[12].wait()
    for t in range(SEQ_SIDE):
        plane = (z + (0, 3, 1, 2)[t]) % SEQ_SIDE
        for k in range(SEQ_SIDE if t > 0 else SEQ_SIDE - 1):
            peer = plane * SEQ_SIDE + (y + (3, 1, 2, 0)[k]) % SEQ_SIDE
            a2a(peer, peer).wait_recv()
        blocks = recv[pl.ds(plane * SEQ_SIDE, SEQ_SIDE)].reshape(SEQ_SIDE * 2 * OWN, BLOCK)

        def transform(j, _):
            lanes = pl.ds(pl.multiple_of(j * 256, 256), 256)
            got = jnp.dot(blocks, high[:, lanes], preferred_element_type=F32)
            got += jnp.dot(blocks, low[:, lanes], preferred_element_type=F32)
            spec[pl.ds(plane * SEQ_SIDE, SEQ_SIDE), :, lanes] = got.reshape(SEQ_SIDE, 2 * OWN, 256)
            return 0

        lax.fori_loop(0, 4, transform, 0)

    def multiply(i, _):
        row = pl.multiple_of(i // 4 * 8, 8)
        lane = pl.multiple_of(i % 4 * 128, 128)
        sign = jnp.where(i % 4 < 2, 1.0, -1.0).astype(F32)
        re, im = pl.ds(lane, 128), pl.ds(lane + BLOCK, 128)
        xs, total_re, total_im = [], [None] * 4, [None] * 4
        for b in range(SEQ):
            xs.append((spec[b, pl.ds(row, 8), re], spec[b, pl.ds(row, 8), im]))
            g_re, g_im = spec[b, pl.ds(row + OWN, 8), re], spec[b, pl.ds(row + OWN, 8), im]
            for m in range(min(b, PARTS) + 1):
                x_re, x_im = xs[b - m]
                add_re = x_re * g_re + x_im * g_im
                add_im = x_re * g_im - x_im * g_re
                total_re[m] = add_re if total_re[m] is None else total_re[m] + add_re
                total_im[m] = add_im if total_im[m] is None else total_im[m] + add_im
        for p in range(PARTS):
            prod[pl.ds(p * OWN + row, 8), re] = total_re[p] + sign * total_im[p + 1]
            prod[pl.ds(p * OWN + row, 8), im] = total_im[p] - sign * total_re[p + 1]
        return 0

    lax.fori_loop(0, 16, multiply, 0)

    weights = prod[...] * (1.0 / BLOCK)
    weights_high = weights.astype(BF16)
    weights_low = (weights - weights_high.astype(F32)).astype(BF16)

    def invert(j, _):
        rows = pl.ds(pl.multiple_of(j * 256, 256), 256)
        got = dot(weights_high, high[rows, :], 1, 1, None)
        got += dot(weights_low, high[rows, :], 1, 1, None)
        got += dot(weights_high, low[rows, :], 1, 1, None)
        for p in range(PARTS):
            lags[:, pl.ds(pl.multiple_of(p * BLOCK + j * 256, 256), 256)] = got[p * OWN : (p + 1) * OWN, :]
        return 0

    lax.fori_loop(0, 2, invert, 0)

    out_delta = lags[...] * envelope[...]
    mine = pl.ds(pl.multiple_of(s * OWN, OWN), OWN)
    head_all[mine, 0:HIDDEN] = dot(out_delta, second_act[...], 1, 1)
    rate_grad = -jnp.sum(out_delta * shaped[...] * feat[0:1, :], axis=1, keepdims=True)
    head_all[mine, HIDDEN:128] = jnp.broadcast_to(rate_grad, (OWN, 128 - HIDDEN))

    def head_copy(slot, peer):
        rows = pl.ds(pl.multiple_of(slot * OWN, OWN), OWN)
        return pltpu.make_async_remote_copy(
            src_ref=head_all.at[rows], dst_ref=head_all.at[rows], send_sem=head_send.at[peer], recv_sem=head_recv.at[slot],
            device_id=(peer, c), device_id_type=MESH,
        )

    for d in range(1, SEQ):
        head_copy(s, (s + d) % SEQ).start()

    second_grad = dot(head_cols, out_delta)
    second_slope = second_grad * second_cos[...]
    second_delta = second_slope * mf_col
    ones = feat[FEATURES : FEATURES + 1, :]
    part[:, 0:HIDDEN] = dot(first_act[...], second_delta, 1, 1)
    first_grad = dot(mw[...], second_delta)
    first_slope = first_grad * first_cos[...]
    first_delta = first_slope * ef_col
    part[0:FEATURE_ROWS, HIDDEN:128] = dot(features, first_delta, 1, 1)
    ones = jnp.broadcast_to(ones, (8, FILTER_LEN))
    part[24:32, HIDDEN:128] = dot(ones, first_slope * first_pre[...], 1, 1)
    part[32:40, HIDDEN:128] = dot(ones, second_delta, 1, 1)
    part[40:48, HIDDEN:128] = dot(ones, second_slope * second_pre[...], 1, 1)
    part[48:64, HIDDEN:128] = jnp.zeros((16, 128 - HIDDEN), F32)

    def sum_copy(slot, peer):
        return pltpu.make_async_remote_copy(
            src_ref=part.at[pl.ds(pl.multiple_of(peer * 8, 8), 8)], dst_ref=sum_recv.at[slot],
            send_sem=sum_send.at[peer], recv_sem=sum_got.at[slot], device_id=(s, peer), device_id_type=MESH,
        )

    for d in range(1, CHAN):
        sum_copy(c, (c + d) % CHAN).start()
    sum_recv[c] = part[pl.ds(pl.multiple_of(c * 8, 8), 8), :]
    for d in range(1, CHAN):
        peer = (c + d) % CHAN
        sum_copy(peer, peer).wait_recv()
    tile[...] = jnp.sum(sum_recv[...], axis=0)

    def tile_copy(slot, peer):
        return pltpu.make_async_remote_copy(
            src_ref=tile, dst_ref=tile_recv.at[slot], send_sem=tile_send.at[peer], recv_sem=tile_got.at[slot],
            device_id=(peer, c), device_id_type=MESH,
        )

    for d in range(1, SEQ):
        tile_copy(s, (s + d) % SEQ).start()
    tile_recv[s] = tile[...]
    for d in range(1, SEQ):
        peer = (s + d) % SEQ
        tile_copy(peer, peer).wait_recv()
    total[c] = jnp.sum(tile_recv[...], axis=0)

    def all_copy(slot, peer):
        return pltpu.make_async_remote_copy(
            src_ref=total.at[slot], dst_ref=total.at[slot], send_sem=all_send.at[peer], recv_sem=all_got.at[slot],
            device_id=(s, peer), device_id_type=MESH,
        )

    for d in range(1, CHAN):
        all_copy(c, (c + d) % CHAN).start()

    for d in range(1, SEQ):
        peer = (s + d) % SEQ
        head_copy(peer, peer).wait_recv()
    turned = head_all[...].T
    hw_out[...] = turned[0:HIDDEN, :]
    dr_out[...] = turned[HIDDEN : HIDDEN + 1, :]

    for d in range(1, CHAN):
        peer = (c + d) % CHAN
        all_copy(peer, peer).wait_recv()
    done = total[...].reshape(HIDDEN, 128)
    mw_out[...] = done[:, 0:HIDDEN]
    ew_out[...] = done[0:FEATURES, HIDDEN:128]
    eb_out[...] = done[FEATURES : FEATURES + 1, HIDDEN:128]
    ef_out[...] = done[24:25, HIDDEN:128]
    mb_out[...] = done[32:33, HIDDEN:128]
    mf_out[...] = done[40:41, HIDDEN:128]

    for d in range(1, SEQ):
        peer = (s + d) % SEQ
        a2a(s, peer).wait_send()
        head_copy(s, peer).wait_send()
        tile_copy(s, peer).wait_send()
    for d in range(1, CHAN):
        peer = (c + d) % CHAN
        sum_copy(c, peer).wait_send()
        all_copy(c, peer).wait_send()


def hand_over(*refs):
    copies = [pltpu.make_async_copy(refs[i], refs[8 + i], refs[16].at[i]) for i in range(8)]
    for copy in copies:
        copy.start()
    for copy in copies:
        copy.wait()


def shards(inputs, out_grad, ew, eb, ef, mw, mb, mf, hw, dr):
    high, low = transform_table()
    row = lambda v: v.reshape(1, -1)
    vmem = pl.BlockSpec(memory_space=pltpu.VMEM)
    anywhere = pl.BlockSpec(memory_space=pl.ANY)
    out = lambda *shape: jax.ShapeDtypeStruct(shape, F32)
    shapes = (
        out(FEATURES, HIDDEN), out(1, HIDDEN), out(1, HIDDEN), out(HIDDEN, HIDDEN), out(1, HIDDEN), out(1, HIDDEN),
        out(HIDDEN, BLOCK), out(1, BLOCK),
    )
    taps = lambda rows: pltpu.VMEM((rows, FILTER_LEN), F32)
    dma = lambda n: pltpu.SemaphoreType.DMA((n,))
    got = pl.pallas_call(
        kernel,
        out_shape=shapes,
        in_specs=[anywhere] * 13,
        out_specs=(vmem,) * 8,
        scratch_shapes=[
            pltpu.VMEM((BLOCK, BLOCK), BF16), pltpu.VMEM((BLOCK, BLOCK), BF16),
            pltpu.VMEM((BLOCK, 2 * BLOCK), BF16), pltpu.VMEM((BLOCK, 2 * BLOCK), BF16),
            taps(FEATURE_ROWS), pltpu.VMEM((FEATURES, HIDDEN), F32), pltpu.VMEM((1, HIDDEN), F32), pltpu.VMEM((1, HIDDEN), F32),
            pltpu.VMEM((HIDDEN, HIDDEN), F32), pltpu.VMEM((1, HIDDEN), F32), pltpu.VMEM((1, HIDDEN), F32),
            pltpu.VMEM((HIDDEN, BLOCK), F32), pltpu.VMEM((1, BLOCK), F32),
            pltpu.VMEM((SEQ, 2 * OWN, BLOCK), BF16), pltpu.VMEM((SEQ, 2 * OWN, BLOCK), BF16),
            pltpu.VMEM((SEQ, 2 * OWN, 2 * BLOCK), F32), pltpu.VMEM((PARTS * OWN, 2 * BLOCK), F32),
            taps(OWN),
            taps(HIDDEN), taps(HIDDEN), taps(HIDDEN), taps(HIDDEN), taps(HIDDEN), taps(HIDDEN), taps(OWN), taps(OWN),
            pltpu.VMEM((BLOCK, 128), F32), pltpu.VMEM((HIDDEN, 128), F32), pltpu.VMEM((CHAN, 8, 128), F32),
            pltpu.VMEM((8, 128), F32), pltpu.VMEM((SEQ, 8, 128), F32), pltpu.VMEM((CHAN, 8, 128), F32),
            dma(13), dma(SEQ), dma(SEQ), dma(SEQ), dma(SEQ), dma(CHAN), dma(CHAN), dma(SEQ), dma(SEQ), dma(CHAN), dma(CHAN),
        ],
        compiler_params=pltpu.CompilerParams(
            collective_id=0, has_side_effects=True, vmem_limit_bytes=VMEM_LIMIT
        ),
    )(
        inputs, out_grad, jnp.asarray(high), jnp.asarray(low), jnp.asarray(tap_table()),
        ew, row(eb), row(ef), mw, row(mb), row(mf), hw, row(dr),
    )
    got = pl.pallas_call(
        hand_over,
        out_shape=shapes,
        in_specs=[anywhere] * 8,
        out_specs=(anywhere,) * 8,
        scratch_shapes=[dma(8)],
    )(*got)
    ew_g, eb_g, ef_g, mw_g, mb_g, mf_g, hw_g, dr_g = got
    flat = lambda v: v.reshape(-1)
    return ew_g, flat(eb_g), flat(ef_g), mw_g, flat(mb_g), flat(mf_g), hw_g, flat(dr_g)


def solution(mesh):
    return jax.shard_map(
        shards,
        mesh=mesh,
        in_specs=(
            P("seq", "chan"), P("seq", "chan"), P(), P(), P(), P(), P(), P(), P(None, "chan"), P("chan"),
        ),
        out_specs=(P(), P(), P(), P(), P(), P(), P(None, "chan"), P("chan")),
        check_vma=False,
    )
```

```python
import math

import jax
import jax.numpy as jnp
import numpy as np
from jax import lax
from jax.experimental import pallas as pl
from jax.experimental.pallas import tpu as pltpu
from jax.sharding import PartitionSpec as P

MESH = pl.DeviceIdType.MESH
EXACT = lax.Precision.HIGHEST
F32 = jnp.float32
BF16 = jnp.bfloat16

FILTER_LEN = 1536
BANDS = 8
FEATURES = 17
FEATURE_ROWS = 24
HIDDEN = 64
BLOCK = 512
SEQ = 16
CHAN = 8
OWN = 32
PARTS = 3
SEQ_SIDE = 4
VMEM_LIMIT = 60 * 1024 * 1024


def transform_table():
    order = np.concatenate([np.arange(0, BLOCK, 2), np.arange(1, BLOCK, 2)])
    turns = (2 * order[None, :] + 1) * np.arange(BLOCK)[:, None] % (4 * BLOCK)
    angle = turns * (2.0 * math.pi / (4 * BLOCK))
    table = np.concatenate([np.cos(angle), -np.sin(angle)], axis=1)
    high = table.astype(BF16)
    low = (table - high.astype(np.float64)).astype(BF16)
    return high, low, np.ascontiguousarray(high.T), np.ascontiguousarray(low.T)


OFFSETS = sorted(
    [(dz, dy) for dz in range(4) for dy in range(4) if dz or dy],
    key=lambda o: -(min(o[0], 4 - o[0]) + min(o[1], 4 - o[1])),
)
GROUPS = (0, 4, 9, 13, 15)


def tap_table():
    taps = np.arange(FILTER_LEN)
    freqs = np.array([max(1, FILTER_LEN // 4 // 2 ** (BANDS - level)) for level in range(1, BANDS + 1)])
    angle = (freqs[:, None] * taps[None, :] % FILTER_LEN) * (2.0 * math.pi / FILTER_LEN)
    table = np.zeros((FEATURE_ROWS, FILTER_LEN), np.float32)
    table[0] = taps / FILTER_LEN
    table[1 : 1 + BANDS] = np.cos(angle)
    table[1 + BANDS : FEATURES] = np.sin(angle)
    table[FEATURES] = 1.0
    return table


def dot(a, b, a_dim=1, b_dim=0, precision=EXACT):
    return lax.dot_general(
        a, b, (((a_dim,), (b_dim,)), ((), ())), precision=precision, preferred_element_type=F32
    )


def halves(v):
    high = v.astype(BF16)
    return high, (v - high.astype(F32)).astype(BF16)


def dot3(a, b, a_dim=1, b_dim=0):
    a_high, a_low = a
    b_high, b_low = b
    return (
        dot(a_high, b_high, a_dim, b_dim, None)
        + dot(a_high, b_low, a_dim, b_dim, None)
        + dot(a_low, b_high, a_dim, b_dim, None)
    )


def sin_cos(a):
    turns = jnp.floor(a * (2.0 / math.pi) + 0.5)
    r = a - turns * 1.5703125
    r = r - turns * 4.837512969970703125e-4
    r = r - turns * 7.549789954891882e-8
    r2 = r * r
    s = r + r * r2 * (-1.6666654611e-1 + r2 * (8.3321608736e-3 + r2 * -1.9515295891e-4))
    c = 1.0 - 0.5 * r2 + r2 * r2 * (4.166664568298827e-2 + r2 * (-1.388731625493765e-3 + r2 * 2.443315711809948e-5))
    q = turns.astype(jnp.int32)
    odd = (q & 1) == 1
    sine = jnp.where(odd, c, s)
    cosine = jnp.where(odd, s, c)
    sine = jnp.where((q & 2) == 2, -sine, sine)
    cosine = jnp.where(((q + 1) & 2) == 2, -cosine, cosine)
    return sine, cosine


def column(row):
    n = row.shape[1]
    hit = lax.broadcasted_iota(jnp.int32, (n, n), 0) == lax.broadcasted_iota(jnp.int32, (n, n), 1)
    return jnp.sum(jnp.where(hit, row, 0.0), axis=1, keepdims=True)


def kernel(
    x_hbm, g_hbm, high_hbm, low_hbm, inv_high_hbm, inv_low_hbm, feat_hbm, ew_hbm, eb_hbm, ef_hbm, mw_hbm, mb_hbm, mf_hbm, hw_hbm, dr_hbm,
    ew_out, eb_out, ef_out, mw_out, mb_out, mf_out, hw_out, dr_out,
    x_in, g_in, high, low, inv_high, inv_low, feat, ew, eb, ef, mw, mb, mf, hw, dr, send, recv, spec, prod, lags,
    first_pre, first_cos, first_act, second_pre, second_cos, second_act, shaped, envelope,
    head_all, part, sum_recv, tile, tile_recv, total,
    local_sem, a2a_send, a2a_recv, head_send, head_recv, sum_send, sum_got, tile_send, tile_got, all_send, all_got,
):
    s = lax.axis_index("seq")
    c = lax.axis_index("chan")
    z = s // SEQ_SIDE
    y = s % SEQ_SIDE

    loads = [
        pltpu.make_async_copy(src, dst, local_sem.at[i])
        for i, (src, dst) in enumerate([
            (x_hbm, x_in), (g_hbm, g_in), (feat_hbm, feat), (ew_hbm, ew), (eb_hbm, eb), (ef_hbm, ef), (mw_hbm, mw),
            (mb_hbm, mb), (mf_hbm, mf), (hw_hbm, hw), (dr_hbm, dr), (high_hbm, high), (low_hbm, low),
            (inv_high_hbm, inv_high), (inv_low_hbm, inv_low),
        ])
    ]
    for load in loads:
        load.start()

    barrier = pltpu.get_barrier_semaphore()
    for d in range(1, SEQ):
        pl.semaphore_signal(barrier, inc=1, device_id=((s + d) % SEQ, c), device_id_type=MESH)
    for d in range(1, CHAN):
        pl.semaphore_signal(barrier, inc=1, device_id=(s, (c + d) % CHAN), device_id_type=MESH)

    def a2a(k, peer):
        return pltpu.make_async_remote_copy(
            src_ref=send.at[peer], dst_ref=recv.at[k], send_sem=a2a_send.at[k], recv_sem=a2a_recv.at[k],
            device_id=(peer, c), device_id_type=MESH,
        )

    def target(k):
        return (z + OFFSETS[k][0]) % SEQ_SIDE * SEQ_SIDE + (y + OFFSETS[k][1]) % SEQ_SIDE

    def source(k):
        return (z - OFFSETS[k][0] + SEQ_SIDE) % SEQ_SIDE * SEQ_SIDE + (y - OFFSETS[k][1] + SEQ_SIDE) % SEQ_SIDE

    loads[0].wait()
    loads[1].wait()
    for t in range(SEQ_SIDE):
        lanes = slice(t * 128, t * 128 + 128)
        rows = slice(t * SEQ_SIDE, (t + 1) * SEQ_SIDE)
        send[rows, 0:OWN, :] = x_in[:, lanes].T.reshape(SEQ_SIDE, OWN, BLOCK)
        send[rows, OWN : 2 * OWN, :] = g_in[:, lanes].T.reshape(SEQ_SIDE, OWN, BLOCK)

    for load in loads[2:11]:
        load.wait()
    ef_col = column(ef[...])
    mf_col = column(mf[...])
    features = feat[...]
    pre = dot(ew[...], features[:FEATURES, :], 0, 0) + column(eb[...])
    act, slope = sin_cos(ef_col * pre)
    first_pre[...] = pre
    first_cos[...] = slope
    first_act[0, 0:HIDDEN, :], first_act[1, 0:HIDDEN, :] = halves(act)
    first_act[0, HIDDEN:, :] = jnp.ones((16, FILTER_LEN), BF16)
    first_act[1, HIDDEN:, :] = jnp.zeros((16, FILTER_LEN), BF16)
    pre = dot(mw[...], act, 0, 0) + column(mb[...])
    act, slope = sin_cos(mf_col * pre)
    second_pre[...] = pre
    second_cos[...] = slope
    second_act[0], second_act[1] = halves(act)
    pick = lax.broadcasted_iota(jnp.int32, (OWN, BLOCK), 1) == lax.broadcasted_iota(jnp.int32, (OWN, BLOCK), 0) + OWN * s
    rates = jnp.sum(jnp.where(pick, dr[...], 0.0), axis=1, keepdims=True)
    picked = jnp.where(pick, 1.0, 0.0).astype(F32)
    head_rows = dot(picked, hw[...], 1, 1)
    head_cols = halves(dot(hw[...], picked, 1, 1))
    shaped[...] = dot(head_rows, act) * features[0:1, :]
    envelope[...] = jnp.exp(-features[0:1, :] * rates)

    pl.semaphore_wait(barrier, SEQ + CHAN - 2)
    for k in range(SEQ - 1):
        a2a(k, target(k)).start()

    recv[SEQ - 1] = send[s]
    loads[11].wait()
    loads[12].wait()
    for group in range(len(GROUPS) - 1):
        slots = list(range(GROUPS[group], GROUPS[group + 1]))
        for k in slots:
            a2a(k, source(k)).wait_recv()
        blocks = recv[slots[0] : slots[-1] + 1].reshape(len(slots) * 2 * OWN, BLOCK)
        owners = [source(k) for k in slots]
        if group == 0:
            blocks = jnp.concatenate([blocks, recv[SEQ - 1]], axis=0)
            owners.append(s)

        def transform(j, _):
            lanes = pl.ds(pl.multiple_of(j * 256, 256), 256)
            got = jnp.dot(blocks, high[:, lanes], preferred_element_type=F32)
            got += jnp.dot(blocks, low[:, lanes], preferred_element_type=F32)
            for i, owner in enumerate(owners):
                spec[owner, :, lanes] = got[i * 2 * OWN : (i + 1) * 2 * OWN, :]
            return 0

        lax.fori_loop(0, 4, transform, 0)
    loads[13].wait()
    loads[14].wait()

    def multiply(i, _):
        row = pl.multiple_of(i // 4 * 8, 8)
        lane = pl.multiple_of(i % 4 * 128, 128)
        sign = jnp.where(i % 4 < 2, 1.0, -1.0).astype(F32)
        re, im = pl.ds(lane, 128), pl.ds(lane + BLOCK, 128)
        xs, total_re, total_im = [], [None] * 4, [None] * 4
        for b in range(SEQ):
            xs.append((spec[b, pl.ds(row, 8), re], spec[b, pl.ds(row, 8), im]))
            g_re, g_im = spec[b, pl.ds(row + OWN, 8), re], spec[b, pl.ds(row + OWN, 8), im]
            for m in range(min(b, PARTS) + 1):
                x_re, x_im = xs[b - m]
                add_re = x_re * g_re + x_im * g_im
                add_im = x_re * g_im - x_im * g_re
                total_re[m] = add_re if total_re[m] is None else total_re[m] + add_re
                total_im[m] = add_im if total_im[m] is None else total_im[m] + add_im
        for p in range(PARTS):
            prod[pl.ds(p * OWN + row, 8), re] = total_re[p] + sign * total_im[p + 1]
            prod[pl.ds(p * OWN + row, 8), im] = total_im[p] - sign * total_re[p + 1]
        return 0

    lax.fori_loop(0, 16, multiply, 0)

    weights_high, weights_low = halves(prod[...] * (1.0 / BLOCK))
    weights = jnp.concatenate([weights_high, weights_low], axis=0)

    def invert(j, _):
        lanes = pl.ds(pl.multiple_of(j * 256, 256), 256)
        both = jnp.dot(weights, inv_high[:, lanes], preferred_element_type=F32)
        got = both[: PARTS * OWN] + both[PARTS * OWN :]
        got += jnp.dot(weights_high, inv_low[:, lanes], preferred_element_type=F32)
        for p in range(PARTS):
            lags[:, pl.ds(pl.multiple_of(p * BLOCK + j * 256, 256), 256)] = got[p * OWN : (p + 1) * OWN, :]
        return 0

    lax.fori_loop(0, 2, invert, 0)

    out_delta = lags[...] * envelope[...]
    delta_halves = halves(out_delta)
    second_acts = second_act[0], second_act[1]
    mine = pl.ds(pl.multiple_of(s * OWN, OWN), OWN)
    head_all[mine, 0:HIDDEN] = dot3(delta_halves, second_acts, 1, 1)
    rate_grad = -jnp.sum(out_delta * shaped[...], axis=1, keepdims=True)
    head_all[mine, HIDDEN:128] = jnp.broadcast_to(rate_grad, (OWN, 128 - HIDDEN))

    def head_copy(slot, peer):
        rows = pl.ds(pl.multiple_of(slot * OWN, OWN), OWN)
        return pltpu.make_async_remote_copy(
            src_ref=head_all.at[rows], dst_ref=head_all.at[rows], send_sem=head_send.at[peer], recv_sem=head_recv.at[slot],
            device_id=(peer, c), device_id_type=MESH,
        )

    for d in range(1, SEQ):
        head_copy(s, (s + d) % SEQ).start()

    second_grad = dot3(head_cols, delta_halves)
    second_slope = second_grad * second_cos[...]
    second_delta = halves(second_slope * mf_col)
    first_slope = dot3(halves(mw[...]), second_delta) * first_cos[...]
    first_delta = halves(first_slope * ef_col)
    mixer_grad = dot3((first_act[0], first_act[1]), second_delta, 1, 1)
    part[:, 0:HIDDEN] = mixer_grad[0:HIDDEN, :]
    part[0:FEATURE_ROWS, HIDDEN:128] = dot3(halves(features), first_delta, 1, 1)
    ones = jnp.ones((8, FILTER_LEN), BF16)
    first_high, first_low = halves(first_slope * first_pre[...])
    part[24:32, HIDDEN:128] = dot(ones, first_high, 1, 1, None) + dot(ones, first_low, 1, 1, None)
    part[32:40, HIDDEN:128] = mixer_grad[HIDDEN : HIDDEN + 8, :]
    second_high, second_low = halves(second_slope * second_pre[...])
    part[40:48, HIDDEN:128] = dot(ones, second_high, 1, 1, None) + dot(ones, second_low, 1, 1, None)
    part[48:64, HIDDEN:128] = jnp.zeros((16, 128 - HIDDEN), F32)

    def everything(ref, count, sem):
        some = ref.at[pl.ds(0, count)]
        pltpu.make_async_remote_copy(
            src_ref=some, dst_ref=some, send_sem=sem.at[0], recv_sem=sem.at[0], device_id=(s, c), device_id_type=MESH
        ).wait_recv()

    def sum_copy(slot, peer):
        return pltpu.make_async_remote_copy(
            src_ref=part.at[pl.ds(pl.multiple_of(peer * 8, 8), 8)], dst_ref=sum_recv.at[slot],
            send_sem=sum_send.at[peer], recv_sem=sum_got.at[0], device_id=(s, peer), device_id_type=MESH,
        )

    for d in range(1, CHAN):
        sum_copy(c, (c + d) % CHAN).start()
    sum_recv[c] = part[pl.ds(pl.multiple_of(c * 8, 8), 8), :]
    everything(sum_recv, CHAN - 1, sum_got)
    tile[...] = jnp.sum(sum_recv[...], axis=0)

    def tile_copy(slot, peer):
        return pltpu.make_async_remote_copy(
            src_ref=tile, dst_ref=tile_recv.at[slot], send_sem=tile_send.at[peer], recv_sem=tile_got.at[0],
            device_id=(peer, c), device_id_type=MESH,
        )

    for d in range(1, SEQ):
        tile_copy(s, (s + d) % SEQ).start()
    tile_recv[s] = tile[...]
    everything(tile_recv, SEQ - 1, tile_got)
    total[c] = jnp.sum(tile_recv[...], axis=0)

    def all_copy(slot, peer):
        return pltpu.make_async_remote_copy(
            src_ref=total.at[slot], dst_ref=total.at[slot], send_sem=all_send.at[peer], recv_sem=all_got.at[0],
            device_id=(s, peer), device_id_type=MESH,
        )

    for d in range(1, CHAN):
        all_copy(c, (c + d) % CHAN).start()

    for d in range(1, SEQ):
        peer = (s + d) % SEQ
        head_copy(peer, peer).wait_recv()
    turned = head_all[...].T
    hw_out[...] = turned[0:HIDDEN, :]
    dr_out[...] = turned[HIDDEN : HIDDEN + 1, :]

    everything(total, CHAN - 1, all_got)
    done = total[...].reshape(HIDDEN, 128)
    mw_out[...] = done[:, 0:HIDDEN]
    ew_out[...] = done[0:FEATURES, HIDDEN:128]
    eb_out[...] = done[FEATURES : FEATURES + 1, HIDDEN:128]
    ef_out[...] = done[24:25, HIDDEN:128]
    mb_out[...] = done[32:33, HIDDEN:128]
    mf_out[...] = done[40:41, HIDDEN:128]

    for d in range(1, SEQ):
        peer = (s + d) % SEQ
        a2a(d - 1, target(d - 1)).wait_send()
        head_copy(s, peer).wait_send()
        tile_copy(s, peer).wait_send()
    for d in range(1, CHAN):
        peer = (c + d) % CHAN
        sum_copy(c, peer).wait_send()
        all_copy(c, peer).wait_send()


def hand_over(*refs):
    for i in range(8):
        refs[8 + i][...] = refs[i][...]


def shards(inputs, out_grad, ew, eb, ef, mw, mb, mf, hw, dr):
    high, low, inv_high, inv_low = transform_table()
    row = lambda v: v.reshape(1, -1)
    vmem = pl.BlockSpec(memory_space=pltpu.VMEM)
    anywhere = pl.BlockSpec(memory_space=pl.ANY)
    out = lambda *shape: jax.ShapeDtypeStruct(shape, F32)
    shapes = (
        out(FEATURES, HIDDEN), out(1, HIDDEN), out(1, HIDDEN), out(HIDDEN, HIDDEN), out(1, HIDDEN), out(1, HIDDEN),
        out(HIDDEN, BLOCK), out(1, BLOCK),
    )
    taps = lambda rows: pltpu.VMEM((rows, FILTER_LEN), F32)
    dma = lambda n: pltpu.SemaphoreType.DMA((n,))
    got = pl.pallas_call(
        kernel,
        out_shape=shapes,
        in_specs=[anywhere] * 15,
        out_specs=(vmem,) * 8,
        scratch_shapes=[
            pltpu.VMEM((BLOCK, BLOCK), BF16), pltpu.VMEM((BLOCK, BLOCK), BF16),
            pltpu.VMEM((BLOCK, 2 * BLOCK), BF16), pltpu.VMEM((BLOCK, 2 * BLOCK), BF16),
            pltpu.VMEM((2 * BLOCK, BLOCK), BF16), pltpu.VMEM((2 * BLOCK, BLOCK), BF16),
            taps(FEATURE_ROWS), pltpu.VMEM((FEATURES, HIDDEN), F32), pltpu.VMEM((1, HIDDEN), F32), pltpu.VMEM((1, HIDDEN), F32),
            pltpu.VMEM((HIDDEN, HIDDEN), F32), pltpu.VMEM((1, HIDDEN), F32), pltpu.VMEM((1, HIDDEN), F32),
            pltpu.VMEM((HIDDEN, BLOCK), F32), pltpu.VMEM((1, BLOCK), F32),
            pltpu.VMEM((SEQ, 2 * OWN, BLOCK), BF16), pltpu.VMEM((SEQ, 2 * OWN, BLOCK), BF16),
            pltpu.VMEM((SEQ, 2 * OWN, 2 * BLOCK), F32), pltpu.VMEM((PARTS * OWN, 2 * BLOCK), F32),
            taps(OWN),
            taps(HIDDEN), taps(HIDDEN), pltpu.VMEM((2, HIDDEN + 16, FILTER_LEN), BF16),
            taps(HIDDEN), taps(HIDDEN), pltpu.VMEM((2, HIDDEN, FILTER_LEN), BF16), taps(OWN), taps(OWN),
            pltpu.VMEM((BLOCK, 128), F32), pltpu.VMEM((HIDDEN, 128), F32), pltpu.VMEM((CHAN, 8, 128), F32),
            pltpu.VMEM((8, 128), F32), pltpu.VMEM((SEQ, 8, 128), F32), pltpu.VMEM((CHAN, 8, 128), F32),
            dma(15), dma(SEQ), dma(SEQ), dma(SEQ), dma(SEQ), dma(CHAN), dma(1), dma(SEQ), dma(1), dma(CHAN), dma(1),
        ],
        compiler_params=pltpu.CompilerParams(
            collective_id=0, has_side_effects=True, vmem_limit_bytes=VMEM_LIMIT
        ),
    )(
        inputs, out_grad, jnp.asarray(high), jnp.asarray(low), jnp.asarray(inv_high), jnp.asarray(inv_low), jnp.asarray(tap_table()),
        ew, row(eb), row(ef), mw, row(mb), row(mf), hw, row(dr),
    )
    got = pl.pallas_call(
        hand_over,
        out_shape=shapes,
        in_specs=[vmem] * 8,
        out_specs=(vmem,) * 8,
    )(*got)
    ew_g, eb_g, ef_g, mw_g, mb_g, mf_g, hw_g, dr_g = got
    flat = lambda v: v.reshape(-1)
    return ew_g, flat(eb_g), flat(ef_g), mw_g, flat(mb_g), flat(mf_g), hw_g, flat(dr_g)


def solution(mesh):
    return jax.shard_map(
        shards,
        mesh=mesh,
        in_specs=(
            P("seq", "chan"), P("seq", "chan"), P(), P(), P(), P(), P(), P(), P(None, "chan"), P("chan"),
        ),
        out_specs=(P(), P(), P(), P(), P(), P(), P(None, "chan"), P("chan")),
        check_vma=False,
    )
```

```python
import math

import jax
import jax.numpy as jnp
import numpy as np
from jax import lax
from jax.experimental import pallas as pl
from jax.experimental.pallas import tpu as pltpu
from jax.sharding import PartitionSpec as P

MESH = pl.DeviceIdType.MESH
EXACT = lax.Precision.HIGHEST
F32 = jnp.float32
BF16 = jnp.bfloat16

FILTER_LEN = 1536
BANDS = 8
FEATURES = 17
FEATURE_ROWS = 24
HIDDEN = 64
BLOCK = 512
SEQ = 16
CHAN = 8
OWN = 32
PARTS = 3
SEQ_SIDE = 4
VMEM_LIMIT = 60 * 1024 * 1024


def transform_table():
    order = np.concatenate([np.arange(0, BLOCK, 2), np.arange(1, BLOCK, 2)])
    turns = (2 * order[None, :] + 1) * np.arange(BLOCK)[:, None] % (4 * BLOCK)
    angle = turns * (2.0 * math.pi / (4 * BLOCK))
    table = np.concatenate([np.cos(angle), -np.sin(angle)], axis=1)
    high = table.astype(BF16)
    low = (table - high.astype(np.float64)).astype(BF16)
    return high, low, np.ascontiguousarray(high.T), np.ascontiguousarray(low.T)


OFFSETS = sorted(
    [(dz, dy) for dz in range(4) for dy in range(4) if dz or dy],
    key=lambda o: -(min(o[0], 4 - o[0]) + min(o[1], 4 - o[1])),
)
GROUPS = (0, 4, 9, 13, 15)


def tap_table():
    taps = np.arange(FILTER_LEN)
    freqs = np.array([max(1, FILTER_LEN // 4 // 2 ** (BANDS - level)) for level in range(1, BANDS + 1)])
    angle = (freqs[:, None] * taps[None, :] % FILTER_LEN) * (2.0 * math.pi / FILTER_LEN)
    table = np.zeros((FEATURE_ROWS, FILTER_LEN), np.float32)
    table[0] = taps / FILTER_LEN
    table[1 : 1 + BANDS] = np.cos(angle)
    table[1 + BANDS : FEATURES] = np.sin(angle)
    table[FEATURES] = 1.0
    return table


def dot(a, b, a_dim=1, b_dim=0, precision=EXACT):
    return lax.dot_general(
        a, b, (((a_dim,), (b_dim,)), ((), ())), precision=precision, preferred_element_type=F32
    )


def halves(v):
    high = v.astype(BF16)
    return high, (v - high.astype(F32)).astype(BF16)


def dot3(a, b, a_dim=1, b_dim=0):
    a_high, a_low = a
    b_high, b_low = b
    return (
        dot(a_high, b_high, a_dim, b_dim, None)
        + dot(a_high, b_low, a_dim, b_dim, None)
        + dot(a_low, b_high, a_dim, b_dim, None)
    )


def sin_cos(a):
    turns = jnp.floor(a * (2.0 / math.pi) + 0.5)
    r = a - turns * 1.5703125
    r = r - turns * 4.837512969970703125e-4
    r = r - turns * 7.549789954891882e-8
    r2 = r * r
    s = r + r * r2 * (-1.6666654611e-1 + r2 * (8.3321608736e-3 + r2 * -1.9515295891e-4))
    c = 1.0 - 0.5 * r2 + r2 * r2 * (4.166664568298827e-2 + r2 * (-1.388731625493765e-3 + r2 * 2.443315711809948e-5))
    q = turns.astype(jnp.int32)
    odd = (q & 1) == 1
    sine = jnp.where(odd, c, s)
    cosine = jnp.where(odd, s, c)
    sine = jnp.where((q & 2) == 2, -sine, sine)
    cosine = jnp.where(((q + 1) & 2) == 2, -cosine, cosine)
    return sine, cosine


def column(row):
    n = row.shape[1]
    hit = lax.broadcasted_iota(jnp.int32, (n, n), 0) == lax.broadcasted_iota(jnp.int32, (n, n), 1)
    return jnp.sum(jnp.where(hit, row, 0.0), axis=1, keepdims=True)


def kernel(
    x_hbm, g_hbm, high_hbm, low_hbm, inv_high_hbm, inv_low_hbm, feat_hbm, ew_hbm, eb_hbm, ef_hbm, mw_hbm, mb_hbm, mf_hbm, hw_hbm, dr_hbm,
    ew_out, eb_out, ef_out, mw_out, mb_out, mf_out, hw_out, dr_out,
    x_in, g_in, high, low, inv_high, inv_low, feat, ew, eb, ef, mw, mb, mf, hw, dr, send, recv, spec, prod, lags,
    first_pre, first_cos, first_act, second_pre, second_cos, second_act, shaped, envelope,
    head_all, packed, chan_recv, chan_total, seq_recv,
    local_sem, a2a_send, a2a_recv, head_send, head_recv, sum_send, sum_got, all_send, all_got,
):
    s = lax.axis_index("seq")
    c = lax.axis_index("chan")
    z = s // SEQ_SIDE
    y = s % SEQ_SIDE

    loads = [
        pltpu.make_async_copy(src, dst, local_sem.at[i])
        for i, (src, dst) in enumerate([
            (x_hbm, x_in), (g_hbm, g_in), (feat_hbm, feat), (ew_hbm, ew), (eb_hbm, eb), (ef_hbm, ef), (mw_hbm, mw),
            (mb_hbm, mb), (mf_hbm, mf), (hw_hbm, hw), (dr_hbm, dr), (high_hbm, high), (low_hbm, low),
            (inv_high_hbm, inv_high), (inv_low_hbm, inv_low),
        ])
    ]
    for load in loads:
        load.start()

    barrier = pltpu.get_barrier_semaphore()
    for d in range(1, SEQ):
        pl.semaphore_signal(barrier, inc=1, device_id=((s + d) % SEQ, c), device_id_type=MESH)
    for d in range(1, CHAN):
        pl.semaphore_signal(barrier, inc=1, device_id=(s, (c + d) % CHAN), device_id_type=MESH)

    def a2a(k, peer):
        return pltpu.make_async_remote_copy(
            src_ref=send.at[peer], dst_ref=recv.at[k], send_sem=a2a_send.at[k], recv_sem=a2a_recv.at[k],
            device_id=(peer, c), device_id_type=MESH,
        )

    def target(k):
        return (z + OFFSETS[k][0]) % SEQ_SIDE * SEQ_SIDE + (y + OFFSETS[k][1]) % SEQ_SIDE

    def source(k):
        return (z - OFFSETS[k][0] + SEQ_SIDE) % SEQ_SIDE * SEQ_SIDE + (y - OFFSETS[k][1] + SEQ_SIDE) % SEQ_SIDE

    loads[0].wait()
    loads[1].wait()
    for t in range(SEQ_SIDE):
        lanes = slice(t * 128, t * 128 + 128)
        rows = slice(t * SEQ_SIDE, (t + 1) * SEQ_SIDE)
        send[rows, 0:OWN, :] = x_in[:, lanes].T.reshape(SEQ_SIDE, OWN, BLOCK)
        send[rows, OWN : 2 * OWN, :] = g_in[:, lanes].T.reshape(SEQ_SIDE, OWN, BLOCK)

    pl.semaphore_wait(barrier, SEQ + CHAN - 2)
    for k in range(SEQ - 1):
        a2a(k, target(k)).start()

    for load in loads[2:11]:
        load.wait()
    ef_col = column(ef[...])
    mf_col = column(mf[...])
    features = feat[...]
    pre = dot(ew[...], features[:FEATURES, :], 0, 0) + column(eb[...])
    act, slope = sin_cos(ef_col * pre)
    first_pre[...] = pre
    first_cos[...] = slope
    first_act[0, 0:HIDDEN, :], first_act[1, 0:HIDDEN, :] = halves(act)
    first_act[0, HIDDEN:, :] = jnp.ones((16, FILTER_LEN), BF16)
    first_act[1, HIDDEN:, :] = jnp.zeros((16, FILTER_LEN), BF16)
    pre = dot(mw[...], act, 0, 0) + column(mb[...])
    act, slope = sin_cos(mf_col * pre)
    second_pre[...] = pre
    second_cos[...] = slope
    second_act[0], second_act[1] = halves(act)
    pick = lax.broadcasted_iota(jnp.int32, (OWN, BLOCK), 1) == lax.broadcasted_iota(jnp.int32, (OWN, BLOCK), 0) + OWN * s
    rates = jnp.sum(jnp.where(pick, dr[...], 0.0), axis=1, keepdims=True)
    picked = jnp.where(pick, 1.0, 0.0).astype(F32)
    head_rows = dot(picked, hw[...], 1, 1)
    head_cols = halves(dot(hw[...], picked, 1, 1))
    shaped[...] = dot(head_rows, act) * features[0:1, :]
    envelope[...] = jnp.exp(-features[0:1, :] * rates)

    recv[SEQ - 1] = send[s]
    loads[11].wait()
    loads[12].wait()
    for group in range(len(GROUPS) - 1):
        slots = list(range(GROUPS[group], GROUPS[group + 1]))
        for k in slots:
            a2a(k, source(k)).wait_recv()
        blocks = recv[slots[0] : slots[-1] + 1].reshape(len(slots) * 2 * OWN, BLOCK)
        owners = [source(k) for k in slots]
        if group == 0:
            blocks = jnp.concatenate([blocks, recv[SEQ - 1]], axis=0)
            owners.append(s)

        for j in range(4):
            lanes = slice(j * 256, j * 256 + 256)
            got = jnp.dot(blocks, high[:, lanes], preferred_element_type=F32)
            got += jnp.dot(blocks, low[:, lanes], preferred_element_type=F32)
            for i, owner in enumerate(owners):
                spec[owner, :, lanes] = got[i * 2 * OWN : (i + 1) * 2 * OWN, :]
    loads[13].wait()
    loads[14].wait()

    def multiply(i, _):
        row = pl.multiple_of(i // 4 * 8, 8)
        lane = pl.multiple_of(i % 4 * 128, 128)
        sign = jnp.where(i % 4 < 2, 1.0, -1.0).astype(F32)
        re, im = pl.ds(lane, 128), pl.ds(lane + BLOCK, 128)
        xs, total_re, total_im = [], [None] * 4, [None] * 4
        for b in range(SEQ):
            xs.append((spec[b, pl.ds(row, 8), re], spec[b, pl.ds(row, 8), im]))
            g_re, g_im = spec[b, pl.ds(row + OWN, 8), re], spec[b, pl.ds(row + OWN, 8), im]
            for m in range(min(b, PARTS) + 1):
                x_re, x_im = xs[b - m]
                add_re = x_re * g_re + x_im * g_im
                add_im = x_re * g_im - x_im * g_re
                total_re[m] = add_re if total_re[m] is None else total_re[m] + add_re
                total_im[m] = add_im if total_im[m] is None else total_im[m] + add_im
        for p in range(PARTS):
            prod[pl.ds(p * OWN + row, 8), re] = total_re[p] + sign * total_im[p + 1]
            prod[pl.ds(p * OWN + row, 8), im] = total_im[p] - sign * total_re[p + 1]
        return 0

    lax.fori_loop(0, 16, multiply, 0)

    weights_high, weights_low = halves(prod[...] * (1.0 / BLOCK))
    weights = jnp.concatenate([weights_high, weights_low], axis=0)

    for j in range(2):
        lanes = slice(j * 256, j * 256 + 256)
        both = jnp.dot(weights, inv_high[:, lanes], preferred_element_type=F32)
        got = both[: PARTS * OWN] + both[PARTS * OWN :]
        got += jnp.dot(weights_high, inv_low[:, lanes], preferred_element_type=F32)
        for p in range(PARTS):
            lags[:, p * BLOCK + j * 256 : p * BLOCK + j * 256 + 256] = got[p * OWN : (p + 1) * OWN, :]

    out_delta = lags[...] * envelope[...]
    delta_halves = halves(out_delta)
    second_acts = second_act[0], second_act[1]
    mine = pl.ds(pl.multiple_of(s * OWN, OWN), OWN)
    head_all[mine, 0:HIDDEN] = dot3(delta_halves, second_acts, 1, 1)
    rate_grad = -jnp.sum(out_delta * shaped[...], axis=1, keepdims=True)
    head_all[mine, HIDDEN:128] = jnp.broadcast_to(rate_grad, (OWN, 128 - HIDDEN))

    def head_copy(slot, peer):
        rows = pl.ds(pl.multiple_of(slot * OWN, OWN), OWN)
        return pltpu.make_async_remote_copy(
            src_ref=head_all.at[rows], dst_ref=head_all.at[rows], send_sem=head_send.at[peer], recv_sem=head_recv.at[slot],
            device_id=(peer, c), device_id_type=MESH,
        )

    for d in range(1, SEQ):
        head_copy(s, (s + d) % SEQ).start()

    second_grad = dot3(head_cols, delta_halves)
    second_slope = second_grad * second_cos[...]
    second_delta = halves(second_slope * mf_col)
    first_slope = dot3(halves(mw[...]), second_delta) * first_cos[...]
    first_delta = halves(first_slope * ef_col)
    mixer_grad = dot3((first_act[0], first_act[1]), second_delta, 1, 1)
    packed[0:32, 0:HIDDEN] = mixer_grad[0:32, :]
    packed[0:32, HIDDEN:128] = mixer_grad[32:HIDDEN, :]
    embed_grad = dot3(halves(features), first_delta, 1, 1)
    packed[32:48, 0:HIDDEN] = embed_grad[0:16, :]
    packed[32:40, HIDDEN:128] = embed_grad[16:24, :]
    ones = jnp.ones((8, FILTER_LEN), BF16)
    first_high, first_low = halves(first_slope * first_pre[...])
    second_high, second_low = halves(second_slope * second_pre[...])
    first_freq = dot(ones, first_high, 1, 1, None) + dot(ones, first_low, 1, 1, None)
    second_freq = dot(ones, second_high, 1, 1, None) + dot(ones, second_low, 1, 1, None)
    packed[40:41, HIDDEN:128] = first_freq[0:1, :]
    packed[41:42, HIDDEN:128] = mixer_grad[HIDDEN : HIDDEN + 1, :]
    packed[42:43, HIDDEN:128] = second_freq[0:1, :]
    packed[43:48, HIDDEN:128] = jnp.zeros((5, 128 - HIDDEN), F32)

    def everything(ref, count, sem):
        some = ref.at[pl.ds(0, count)]
        pltpu.make_async_remote_copy(
            src_ref=some, dst_ref=some, send_sem=sem.at[0], recv_sem=sem.at[0], device_id=(s, c), device_id_type=MESH
        ).wait_recv()

    def sum_copy(slot, peer):
        return pltpu.make_async_remote_copy(
            src_ref=packed, dst_ref=chan_recv.at[slot], send_sem=sum_send.at[peer], recv_sem=sum_got.at[0],
            device_id=(s, peer), device_id_type=MESH,
        )

    for d in range(1, CHAN):
        sum_copy(c, (c + d) % CHAN).start()
    chan_recv[c] = packed[...]
    everything(chan_recv, CHAN - 1, sum_got)
    chan_total[...] = jnp.sum(chan_recv[...], axis=0)

    def all_copy(slot, peer):
        return pltpu.make_async_remote_copy(
            src_ref=chan_total, dst_ref=seq_recv.at[slot], send_sem=all_send.at[peer], recv_sem=all_got.at[0],
            device_id=(peer, c), device_id_type=MESH,
        )

    for k in range(SEQ - 1):
        all_copy(s, target(k)).start()
    seq_recv[s] = chan_total[...]

    for d in range(1, SEQ):
        peer = (s + d) % SEQ
        head_copy(peer, peer).wait_recv()
    turned = head_all[...].T
    hw_out[...] = turned[0:HIDDEN, :]
    dr_out[...] = turned[HIDDEN : HIDDEN + 1, :]

    everything(seq_recv, SEQ - 1, all_got)
    done = jnp.sum(seq_recv[...], axis=0)
    mw_out[0:32, :] = done[0:32, 0:HIDDEN]
    mw_out[32:HIDDEN, :] = done[0:32, HIDDEN:128]
    ew_out[0:16, :] = done[32:48, 0:HIDDEN]
    ew_out[16:17, :] = done[32:33, HIDDEN:128]
    eb_out[...] = done[33:34, HIDDEN:128]
    ef_out[...] = done[40:41, HIDDEN:128]
    mb_out[...] = done[41:42, HIDDEN:128]
    mf_out[...] = done[42:43, HIDDEN:128]

    for d in range(1, SEQ):
        peer = (s + d) % SEQ
        a2a(d - 1, target(d - 1)).wait_send()
        head_copy(s, peer).wait_send()
        all_copy(s, peer).wait_send()
    for d in range(1, CHAN):
        peer = (c + d) % CHAN
        sum_copy(c, peer).wait_send()


def hand_over(*refs):
    for i in range(8):
        refs[8 + i][...] = refs[i][...]


def shards(inputs, out_grad, ew, eb, ef, mw, mb, mf, hw, dr):
    high, low, inv_high, inv_low = transform_table()
    row = lambda v: v.reshape(1, -1)
    vmem = pl.BlockSpec(memory_space=pltpu.VMEM)
    anywhere = pl.BlockSpec(memory_space=pl.ANY)
    out = lambda *shape: jax.ShapeDtypeStruct(shape, F32)
    shapes = (
        out(FEATURES, HIDDEN), out(1, HIDDEN), out(1, HIDDEN), out(HIDDEN, HIDDEN), out(1, HIDDEN), out(1, HIDDEN),
        out(HIDDEN, BLOCK), out(1, BLOCK),
    )
    taps = lambda rows: pltpu.VMEM((rows, FILTER_LEN), F32)
    dma = lambda n: pltpu.SemaphoreType.DMA((n,))
    got = pl.pallas_call(
        kernel,
        out_shape=shapes,
        in_specs=[anywhere] * 15,
        out_specs=(vmem,) * 8,
        scratch_shapes=[
            pltpu.VMEM((BLOCK, BLOCK), BF16), pltpu.VMEM((BLOCK, BLOCK), BF16),
            pltpu.VMEM((BLOCK, 2 * BLOCK), BF16), pltpu.VMEM((BLOCK, 2 * BLOCK), BF16),
            pltpu.VMEM((2 * BLOCK, BLOCK), BF16), pltpu.VMEM((2 * BLOCK, BLOCK), BF16),
            taps(FEATURE_ROWS), pltpu.VMEM((FEATURES, HIDDEN), F32), pltpu.VMEM((1, HIDDEN), F32), pltpu.VMEM((1, HIDDEN), F32),
            pltpu.VMEM((HIDDEN, HIDDEN), F32), pltpu.VMEM((1, HIDDEN), F32), pltpu.VMEM((1, HIDDEN), F32),
            pltpu.VMEM((HIDDEN, BLOCK), F32), pltpu.VMEM((1, BLOCK), F32),
            pltpu.VMEM((SEQ, 2 * OWN, BLOCK), BF16), pltpu.VMEM((SEQ, 2 * OWN, BLOCK), BF16),
            pltpu.VMEM((SEQ, 2 * OWN, 2 * BLOCK), F32), pltpu.VMEM((PARTS * OWN, 2 * BLOCK), F32),
            taps(OWN),
            taps(HIDDEN), taps(HIDDEN), pltpu.VMEM((2, HIDDEN + 16, FILTER_LEN), BF16),
            taps(HIDDEN), taps(HIDDEN), pltpu.VMEM((2, HIDDEN, FILTER_LEN), BF16), taps(OWN), taps(OWN),
            pltpu.VMEM((BLOCK, 128), F32), pltpu.VMEM((48, 128), F32), pltpu.VMEM((CHAN, 48, 128), F32),
            pltpu.VMEM((48, 128), F32), pltpu.VMEM((SEQ, 48, 128), F32),
            dma(15), dma(SEQ), dma(SEQ), dma(SEQ), dma(SEQ), dma(CHAN), dma(1), dma(SEQ), dma(1),
        ],
        compiler_params=pltpu.CompilerParams(
            collective_id=0, has_side_effects=True, vmem_limit_bytes=VMEM_LIMIT
        ),
    )(
        inputs, out_grad, jnp.asarray(high), jnp.asarray(low), jnp.asarray(inv_high), jnp.asarray(inv_low), jnp.asarray(tap_table()),
        ew, row(eb), row(ef), mw, row(mb), row(mf), hw, row(dr),
    )
    got = pl.pallas_call(
        hand_over,
        out_shape=shapes,
        in_specs=[vmem] * 8,
        out_specs=(vmem,) * 8,
    )(*got)
    ew_g, eb_g, ef_g, mw_g, mb_g, mf_g, hw_g, dr_g = got
    flat = lambda v: v.reshape(-1)
    return ew_g, flat(eb_g), flat(ef_g), mw_g, flat(mb_g), flat(mf_g), hw_g, flat(dr_g)


def solution(mesh):
    return jax.shard_map(
        shards,
        mesh=mesh,
        in_specs=(
            P("seq", "chan"), P("seq", "chan"), P(), P(), P(), P(), P(), P(), P(None, "chan"), P("chan"),
        ),
        out_specs=(P(), P(), P(), P(), P(), P(), P(None, "chan"), P("chan")),
        check_vma=False,
    )
```

```python
import math

import jax
import jax.numpy as jnp
import numpy as np
from jax import lax
from jax.experimental import pallas as pl
from jax.experimental.pallas import tpu as pltpu
from jax.sharding import PartitionSpec as P

MESH = pl.DeviceIdType.MESH
EXACT = lax.Precision.HIGHEST
F32 = jnp.float32
BF16 = jnp.bfloat16

FILTER_LEN = 1536
BANDS = 8
FEATURES = 17
FEATURE_ROWS = 24
HIDDEN = 64
BLOCK = 512
SEQ = 16
CHAN = 8
OWN = 32
PARTS = 3
SEQ_SIDE = 4
TILES = 4
VMEM_LIMIT = 60 * 1024 * 1024


def transform_table():
    order = np.concatenate([np.arange(0, BLOCK, 2), np.arange(1, BLOCK, 2)])
    turns = (2 * order[None, :] + 1) * np.arange(BLOCK)[:, None] % (4 * BLOCK)
    angle = turns * (2.0 * math.pi / (4 * BLOCK))
    table = np.stack([np.cos(angle).reshape(BLOCK, TILES, 128), -np.sin(angle).reshape(BLOCK, TILES, 128)], axis=2)
    table = table.reshape(BLOCK, 2 * BLOCK)
    high = table.astype(BF16)
    low = (table - high.astype(np.float64)).astype(BF16)
    inverse = lambda t: np.ascontiguousarray((t.astype(np.float32) / BLOCK).astype(BF16).T)
    return high, low, inverse(high), inverse(low)


OFFSETS = sorted(
    [(dz, dy) for dz in range(4) for dy in range(4) if dz or dy],
    key=lambda o: -(min(o[0], 4 - o[0]) + min(o[1], 4 - o[1])),
)
GROUPS = (0, 5, 10, 13, 15)


def tap_table():
    taps = np.arange(FILTER_LEN)
    freqs = np.array([max(1, FILTER_LEN // 4 // 2 ** (BANDS - level)) for level in range(1, BANDS + 1)])
    angle = (freqs[:, None] * taps[None, :] % FILTER_LEN) * (2.0 * math.pi / FILTER_LEN)
    table = np.zeros((FEATURE_ROWS, FILTER_LEN), np.float32)
    table[0] = taps / FILTER_LEN
    table[1 : 1 + BANDS] = np.cos(angle)
    table[1 + BANDS : FEATURES] = np.sin(angle)
    table[FEATURES] = 1.0
    return table


def dot(a, b, a_dim=1, b_dim=0, precision=EXACT):
    return lax.dot_general(
        a, b, (((a_dim,), (b_dim,)), ((), ())), precision=precision, preferred_element_type=F32
    )


def halves(v):
    high = v.astype(BF16)
    return high, (v - high.astype(F32)).astype(BF16)


def dot3(a, b, a_dim=1, b_dim=0):
    a_high, a_low = a
    b_high, b_low = b
    return (
        dot(a_high, b_high, a_dim, b_dim, None)
        + dot(a_high, b_low, a_dim, b_dim, None)
        + dot(a_low, b_high, a_dim, b_dim, None)
    )


def sin_cos(a):
    turns = jnp.floor(a * (2.0 / math.pi) + 0.5)
    r = a - turns * 1.5703125
    r = r - turns * 4.837512969970703125e-4
    r = r - turns * 7.549789954891882e-8
    r2 = r * r
    s = r + r * r2 * (-1.6666654611e-1 + r2 * (8.3321608736e-3 + r2 * -1.9515295891e-4))
    c = 1.0 - 0.5 * r2 + r2 * r2 * (4.166664568298827e-2 + r2 * (-1.388731625493765e-3 + r2 * 2.443315711809948e-5))
    q = turns.astype(jnp.int32)
    odd = (q & 1) == 1
    sine = jnp.where(odd, c, s)
    cosine = jnp.where(odd, s, c)
    sine = jnp.where((q & 2) == 2, -sine, sine)
    cosine = jnp.where(((q + 1) & 2) == 2, -cosine, cosine)
    return sine, cosine


def column(row):
    n = row.shape[1]
    hit = lax.broadcasted_iota(jnp.int32, (n, n), 0) == lax.broadcasted_iota(jnp.int32, (n, n), 1)
    return jnp.sum(jnp.where(hit, row, 0.0), axis=1, keepdims=True)


def kernel(
    x_hbm, g_hbm, high_hbm, low_hbm, inv_high_hbm, inv_low_hbm, feat_hbm, ew_hbm, eb_hbm, ef_hbm, mw_hbm, mb_hbm, mf_hbm, hw_hbm, dr_hbm,
    ew_out, eb_out, ef_out, mw_out, mb_out, mf_out, hw_out, dr_out,
    x_in, g_in, high, low, inv_high, inv_low, feat, ew, eb, ef, mw, mb, mf, hw, dr, send, recv,
    spec_0, spec_1, spec_2, spec_3,
    first_pre, first_cos, first_act, second_pre, second_cos, second_act, shaped, envelope,
    head_all, head_turned, packed, chan_recv, chan_total, seq_recv, done,
    local_sem, a2a_send, a2a_recv, head_send, head_recv, sum_send, sum_got, all_send, all_got,
    swap_sem, out_sem,
):
    spec = spec_0, spec_1, spec_2, spec_3
    s = lax.axis_index("seq")
    c = lax.axis_index("chan")
    z = s // SEQ_SIDE
    y = s % SEQ_SIDE

    loads = [
        pltpu.make_async_copy(src, dst, local_sem.at[i])
        for i, (src, dst) in enumerate([
            (x_hbm, x_in), (g_hbm, g_in), (feat_hbm, feat), (ew_hbm, ew), (eb_hbm, eb), (ef_hbm, ef), (mw_hbm, mw),
            (mb_hbm, mb), (mf_hbm, mf), (hw_hbm, hw), (dr_hbm, dr), (high_hbm, high), (low_hbm, low),
            (inv_high_hbm, inv_high), (inv_low_hbm, inv_low),
        ])
    ]
    for load in loads:
        load.start()

    barrier = pltpu.get_barrier_semaphore()
    for d in range(1, SEQ):
        pl.semaphore_signal(barrier, inc=1, device_id=((s + d) % SEQ, c), device_id_type=MESH)
    for d in range(1, CHAN):
        pl.semaphore_signal(barrier, inc=1, device_id=(s, (c + d) % CHAN), device_id_type=MESH)

    def a2a(k, peer):
        return pltpu.make_async_remote_copy(
            src_ref=send.at[peer], dst_ref=recv.at[k], send_sem=a2a_send.at[k], recv_sem=a2a_recv.at[k],
            device_id=(peer, c), device_id_type=MESH,
        )

    def target(k):
        return (z + OFFSETS[k][0]) % SEQ_SIDE * SEQ_SIDE + (y + OFFSETS[k][1]) % SEQ_SIDE

    def source(k):
        return (z - OFFSETS[k][0] + SEQ_SIDE) % SEQ_SIDE * SEQ_SIDE + (y - OFFSETS[k][1] + SEQ_SIDE) % SEQ_SIDE

    loads[0].wait()
    loads[1].wait()
    for t in range(SEQ_SIDE):
        lanes = slice(t * 128, t * 128 + 128)
        rows = slice(t * SEQ_SIDE, (t + 1) * SEQ_SIDE)
        send[rows, 0:OWN, :] = x_in[:, lanes].T.reshape(SEQ_SIDE, OWN, BLOCK)
        send[rows, OWN : 2 * OWN, :] = g_in[:, lanes].T.reshape(SEQ_SIDE, OWN, BLOCK)

    pl.semaphore_wait(barrier, SEQ + CHAN - 2)
    for k in range(SEQ - 1):
        a2a(k, target(k)).start()

    for load in loads[2:11]:
        load.wait()
    ef_col = column(ef[...])
    mf_col = column(mf[...])
    features = feat[...]
    pre = dot(ew[...], features[:FEATURES, :], 0, 0) + column(eb[...])
    act, slope = sin_cos(ef_col * pre)
    first_pre[...] = pre
    first_cos[...] = slope
    first_act[0, 0:HIDDEN, :], first_act[1, 0:HIDDEN, :] = halves(act)
    first_act[0, HIDDEN:, :] = jnp.ones((16, FILTER_LEN), BF16)
    first_act[1, HIDDEN:, :] = jnp.zeros((16, FILTER_LEN), BF16)
    pre = dot(mw[...], act, 0, 0) + column(mb[...])
    act, slope = sin_cos(mf_col * pre)
    second_pre[...] = pre
    second_cos[...] = slope
    second_act[0], second_act[1] = halves(act)
    pick = lax.broadcasted_iota(jnp.int32, (OWN, BLOCK), 1) == lax.broadcasted_iota(jnp.int32, (OWN, BLOCK), 0) + OWN * s
    rates = jnp.sum(jnp.where(pick, dr[...], 0.0), axis=1, keepdims=True)
    picked = jnp.where(pick, 1.0, 0.0).astype(F32)
    head_rows = dot(picked, hw[...], 1, 1)
    head_cols = halves(dot(hw[...], picked, 1, 1))
    shaped[...] = dot(head_rows, act) * features[0:1, :]
    envelope[...] = jnp.exp(-features[0:1, :] * rates)

    def transform(tile, blocks, owners):
        lanes = slice(tile * 256, tile * 256 + 256)
        got = jnp.dot(blocks, high[:, lanes], preferred_element_type=F32)
        got += jnp.dot(blocks, low[:, lanes], preferred_element_type=F32)
        for i, owner in enumerate(owners):
            spec[tile][owner, :, :] = got[i * 2 * OWN : (i + 1) * 2 * OWN, :]

    def multiply(tile):
        parts_re, parts_im = [[] for _ in range(PARTS)], [[] for _ in range(PARTS)]
        for row in range(0, OWN, 8):
            xs, total_re, total_im = [], [None] * 4, [None] * 4
            for b in range(SEQ):
                x_rows, g_rows = slice(row, row + 8), slice(OWN + row, OWN + row + 8)
                xs.append((spec[tile][b, x_rows, 0:128], spec[tile][b, x_rows, 128:256]))
                g_re, g_im = spec[tile][b, g_rows, 0:128], spec[tile][b, g_rows, 128:256]
                for m in range(min(b, PARTS) + 1):
                    x_re, x_im = xs[b - m]
                    add_re = x_re * g_re + x_im * g_im
                    add_im = x_re * g_im - x_im * g_re
                    total_re[m] = add_re if total_re[m] is None else total_re[m] + add_re
                    total_im[m] = add_im if total_im[m] is None else total_im[m] + add_im
            for p in range(PARTS):
                if tile < TILES // 2:
                    parts_re[p].append(total_re[p] + total_im[p + 1])
                    parts_im[p].append(total_im[p] - total_re[p + 1])
                else:
                    parts_re[p].append(total_re[p] - total_im[p + 1])
                    parts_im[p].append(total_im[p] + total_re[p + 1])
        join = lambda parts: jnp.concatenate([v for part in parts for v in part], axis=0)
        return jnp.concatenate([join(parts_re), join(parts_im)], axis=1)

    recv[SEQ - 1] = send[s]
    loads[11].wait()
    loads[12].wait()
    for group in range(len(GROUPS) - 1):
        slots = list(range(GROUPS[group], GROUPS[group + 1]))
        for k in slots:
            a2a(k, source(k)).wait_recv()
        blocks = recv[slots[0] : slots[-1] + 1].reshape(len(slots) * 2 * OWN, BLOCK)
        owners = [source(k) for k in slots]
        if group == 0:
            blocks = jnp.concatenate([blocks, recv[SEQ - 1]], axis=0)
            owners.append(s)

        if group < len(GROUPS) - 2:
            for tile in range(TILES):
                transform(tile, blocks, owners)
    loads[13].wait()
    loads[14].wait()

    total = None
    for tile in range(TILES):
        transform(tile, blocks, owners)
        weights_high, weights_low = halves(multiply(tile))
        weights = jnp.concatenate([weights_high, weights_low], axis=0)
        rows = slice(tile * 256, tile * 256 + 256)
        both = jnp.dot(weights, inv_high[rows, :], preferred_element_type=F32)
        share = both[: PARTS * OWN] + both[PARTS * OWN :]
        share += jnp.dot(weights_high, inv_low[rows, :], preferred_element_type=F32)
        total = share if total is None else total + share
    lags = jnp.concatenate([total[p * OWN : (p + 1) * OWN, :] for p in range(PARTS)], axis=1)

    out_delta = lags * envelope[...]
    delta_halves = halves(out_delta)
    second_acts = second_act[0], second_act[1]
    mine = pl.ds(pl.multiple_of(s * OWN, OWN), OWN)
    head_all[mine, 0:HIDDEN] = dot3(delta_halves, second_acts, 1, 1)
    rate_grad = -jnp.sum(out_delta * shaped[...], axis=1, keepdims=True)
    head_all[mine, HIDDEN:128] = jnp.broadcast_to(rate_grad, (OWN, 128 - HIDDEN))

    def head_copy(slot, peer):
        rows = pl.ds(pl.multiple_of(slot * OWN, OWN), OWN)
        return pltpu.make_async_remote_copy(
            src_ref=head_all.at[rows], dst_ref=head_all.at[rows], send_sem=head_send.at[peer], recv_sem=head_recv.at[slot],
            device_id=(peer, c), device_id_type=MESH,
        )

    for d in range(1, SEQ):
        head_copy(s, (s + d) % SEQ).start()

    second_grad = dot3(head_cols, delta_halves)
    second_slope = second_grad * second_cos[...]
    second_delta = halves(second_slope * mf_col)
    first_slope = dot3(halves(mw[...]), second_delta) * first_cos[...]
    first_delta = halves(first_slope * ef_col)
    mixer_grad = dot3((first_act[0], first_act[1]), second_delta, 1, 1)
    embed_grad = dot3(halves(features), first_delta, 1, 1)
    ones = jnp.ones((8, FILTER_LEN), BF16)
    first_high, first_low = halves(first_slope * first_pre[...])
    second_high, second_low = halves(second_slope * second_pre[...])
    first_freq = dot(ones, first_high, 1, 1, None) + dot(ones, first_low, 1, 1, None)
    second_freq = dot(ones, second_high, 1, 1, None) + dot(ones, second_low, 1, 1, None)
    packed[0, :, 0:HIDDEN] = mixer_grad[0:24, :]
    packed[0, 0:16, HIDDEN:128] = mixer_grad[24:40, :]
    packed[0, 16:24, HIDDEN:128] = embed_grad[16:24, :]
    packed[1, :, 0:HIDDEN] = mixer_grad[40:64, :]
    packed[1, 0:16, HIDDEN:128] = embed_grad[0:16, :]
    packed[1, 16:17, HIDDEN:128] = first_freq[0:1, :]
    packed[1, 17:18, HIDDEN:128] = mixer_grad[HIDDEN : HIDDEN + 1, :]
    packed[1, 18:19, HIDDEN:128] = second_freq[0:1, :]
    packed[1, 19:24, HIDDEN:128] = jnp.zeros((5, 128 - HIDDEN), F32)

    def everything(ref, count, sem):
        some = ref.at[pl.ds(0, count)]
        return pltpu.make_async_remote_copy(
            src_ref=some, dst_ref=some, send_sem=sem.at[0], recv_sem=sem.at[0], device_id=(s, c), device_id_type=MESH
        )

    core = c % 2
    for d in range(1, CHAN):
        peer = (c + d) % CHAN
        pltpu.make_async_remote_copy(
            src_ref=packed.at[peer % 2], dst_ref=chan_recv.at[c], send_sem=sum_send.at[0], recv_sem=sum_got.at[0],
            device_id=(s, peer), device_id_type=MESH,
        ).start()
    chan_recv[c] = packed[core]
    everything(chan_recv, CHAN - 1, sum_got).wait_recv()
    chan_total[...] = jnp.sum(chan_recv[...], axis=0)
    for k in range(SEQ - 1):
        pltpu.make_async_remote_copy(
            src_ref=chan_total, dst_ref=seq_recv.at[s], send_sem=all_send.at[0], recv_sem=all_got.at[0],
            device_id=(target(k), c), device_id_type=MESH,
        ).start()
    seq_recv[s] = chan_total[...]

    for d in range(1, SEQ):
        peer = (s + d) % SEQ
        head_copy(peer, peer).wait_recv()
    head_turned[...] = head_all[...].T
    head_out = [
        pltpu.make_async_copy(head_turned.at[0:HIDDEN], hw_out, out_sem.at[0]),
        pltpu.make_async_copy(head_turned.at[HIDDEN : HIDDEN + 8], dr_out, out_sem.at[1]),
    ]
    for copy in head_out:
        copy.start()
    for d in range(1, SEQ):
        a2a(d - 1, target(d - 1)).wait_send()
        head_copy(s, (s + d) % SEQ).wait_send()
    everything(chan_recv, CHAN - 1, sum_send).wait_send()

    everything(seq_recv, SEQ - 1, all_got).wait_recv()
    done[core] = jnp.sum(seq_recv[...], axis=0)
    swap = pltpu.make_async_remote_copy(
        src_ref=done.at[core], dst_ref=done.at[core], send_sem=swap_sem.at[0], recv_sem=swap_sem.at[1],
        device_id=(s, c + 1 - 2 * core), device_id_type=MESH,
    )
    swap.start()
    everything(seq_recv, SEQ - 1, all_send).wait_send()
    for copy in head_out:
        copy.wait()
    swap.wait()
    mw_out[0:24, :] = done[0, :, 0:HIDDEN]
    mw_out[24:40, :] = done[0, 0:16, HIDDEN:128]
    mw_out[40:64, :] = done[1, :, 0:HIDDEN]
    ew_out[0:16, :] = done[1, 0:16, HIDDEN:128]
    ew_out[16:17, :] = done[0, 16:17, HIDDEN:128]
    eb_out[...] = done[0, 17:18, HIDDEN:128]
    ef_out[...] = done[1, 16:17, HIDDEN:128]
    mb_out[...] = done[1, 17:18, HIDDEN:128]
    mf_out[...] = done[1, 18:19, HIDDEN:128]


def hand_over(*refs):
    for i in range(7):
        refs[8 + i][...] = refs[i][...]
    refs[15][...] = refs[7][0:1, :]


def shards(inputs, out_grad, ew, eb, ef, mw, mb, mf, hw, dr):
    high, low, inv_high, inv_low = transform_table()
    row = lambda v: v.reshape(1, -1)
    vmem = pl.BlockSpec(memory_space=pltpu.VMEM)
    anywhere = pl.BlockSpec(memory_space=pl.ANY)
    out = lambda *shape: jax.ShapeDtypeStruct(shape, F32)
    shapes = (
        out(FEATURES, HIDDEN), out(1, HIDDEN), out(1, HIDDEN), out(HIDDEN, HIDDEN), out(1, HIDDEN), out(1, HIDDEN),
        out(HIDDEN, BLOCK), out(1, BLOCK),
    )
    taps = lambda rows: pltpu.VMEM((rows, FILTER_LEN), F32)
    dma = lambda n: pltpu.SemaphoreType.DMA((n,))
    got = pl.pallas_call(
        kernel,
        out_shape=shapes[:7] + (out(8, BLOCK),),
        in_specs=[anywhere] * 15,
        out_specs=(vmem,) * 6 + (anywhere,) * 2,
        scratch_shapes=[
            pltpu.VMEM((BLOCK, BLOCK), BF16), pltpu.VMEM((BLOCK, BLOCK), BF16),
            pltpu.VMEM((BLOCK, 2 * BLOCK), BF16), pltpu.VMEM((BLOCK, 2 * BLOCK), BF16),
            pltpu.VMEM((2 * BLOCK, BLOCK), BF16), pltpu.VMEM((2 * BLOCK, BLOCK), BF16),
            taps(FEATURE_ROWS), pltpu.VMEM((FEATURES, HIDDEN), F32), pltpu.VMEM((1, HIDDEN), F32), pltpu.VMEM((1, HIDDEN), F32),
            pltpu.VMEM((HIDDEN, HIDDEN), F32), pltpu.VMEM((1, HIDDEN), F32), pltpu.VMEM((1, HIDDEN), F32),
            pltpu.VMEM((HIDDEN, BLOCK), F32), pltpu.VMEM((1, BLOCK), F32),
            pltpu.VMEM((SEQ, 2 * OWN, BLOCK), BF16), pltpu.VMEM((SEQ, 2 * OWN, BLOCK), BF16),
            *[pltpu.VMEM((SEQ, 2 * OWN, 256), F32)] * TILES,
            taps(HIDDEN), taps(HIDDEN), pltpu.VMEM((2, HIDDEN + 16, FILTER_LEN), BF16),
            taps(HIDDEN), taps(HIDDEN), pltpu.VMEM((2, HIDDEN, FILTER_LEN), BF16), taps(OWN), taps(OWN),
            pltpu.VMEM((BLOCK, 128), F32), pltpu.VMEM((128, BLOCK), F32), pltpu.VMEM((2, 24, 128), F32),
            pltpu.VMEM((CHAN, 24, 128), F32), pltpu.VMEM((24, 128), F32), pltpu.VMEM((SEQ, 24, 128), F32),
            pltpu.VMEM((2, 24, 128), F32),
            dma(15), dma(SEQ), dma(SEQ), dma(SEQ), dma(SEQ), dma(1), dma(1), dma(1), dma(1), dma(2), dma(2),
        ],
        compiler_params=pltpu.CompilerParams(
            collective_id=0, has_side_effects=True, vmem_limit_bytes=VMEM_LIMIT
        ),
    )(
        inputs, out_grad, jnp.asarray(high), jnp.asarray(low), jnp.asarray(inv_high), jnp.asarray(inv_low), jnp.asarray(tap_table()),
        ew, row(eb), row(ef), mw, row(mb), row(mf), hw, row(dr),
    )
    got = pl.pallas_call(
        hand_over,
        out_shape=shapes,
        in_specs=[vmem] * 8,
        out_specs=(vmem,) * 8,
    )(*got)
    ew_g, eb_g, ef_g, mw_g, mb_g, mf_g, hw_g, dr_g = got
    flat = lambda v: v.reshape(-1)
    return ew_g, flat(eb_g), flat(ef_g), mw_g, flat(mb_g), flat(mf_g), hw_g, flat(dr_g)


def solution(mesh):
    return jax.shard_map(
        shards,
        mesh=mesh,
        in_specs=(
            P("seq", "chan"), P("seq", "chan"), P(), P(), P(), P(), P(), P(), P(None, "chan"), P("chan"),
        ),
        out_specs=(P(), P(), P(), P(), P(), P(), P(None, "chan"), P("chan")),
        check_vma=False,
    )
```

```python
import math

import jax
import jax.numpy as jnp
import numpy as np
from jax import lax
from jax.experimental import pallas as pl
from jax.experimental.pallas import tpu as pltpu
from jax.sharding import PartitionSpec as P

MESH = pl.DeviceIdType.MESH
EXACT = lax.Precision.HIGHEST
F32 = jnp.float32
BF16 = jnp.bfloat16

FILTER_LEN = 1536
BANDS = 8
FEATURES = 17
FEATURE_ROWS = 24
HIDDEN = 64
BLOCK = 512
SEQ = 16
CHAN = 8
OWN = 32
PARTS = 3
SEQ_SIDE = 4
TILES = 4
VMEM_LIMIT = 60 * 1024 * 1024


def transform_table():
    order = np.concatenate([np.arange(0, BLOCK, 2), np.arange(1, BLOCK, 2)])
    turns = (2 * order[None, :] + 1) * np.arange(BLOCK)[:, None] % (4 * BLOCK)
    angle = turns * (2.0 * math.pi / (4 * BLOCK))
    table = np.stack([np.cos(angle).reshape(BLOCK, TILES, 128), -np.sin(angle).reshape(BLOCK, TILES, 128)], axis=2)
    table = table.reshape(BLOCK, 2 * BLOCK)
    high = table.astype(BF16)
    low = (table - high.astype(np.float64)).astype(BF16)
    inverse = lambda t: np.ascontiguousarray((t.astype(np.float32) / BLOCK).astype(BF16).T)
    return high, low, inverse(high), inverse(low)


STRAIGHT = 6
OFFSETS = [(2, 0), (0, 2), (0, 1), (0, 3), (1, 0), (3, 0)]
OFFSETS += [(2, 2), (1, 2), (2, 1), (2, 3), (3, 2), (1, 1), (1, 3), (3, 1), (3, 3)]
GROUPS = (0, 6, 10, 13, 15)


def tap_table():
    taps = np.arange(FILTER_LEN)
    freqs = np.array([max(1, FILTER_LEN // 4 // 2 ** (BANDS - level)) for level in range(1, BANDS + 1)])
    angle = (freqs[:, None] * taps[None, :] % FILTER_LEN) * (2.0 * math.pi / FILTER_LEN)
    table = np.zeros((FEATURE_ROWS, FILTER_LEN), np.float32)
    table[0] = taps / FILTER_LEN
    table[1 : 1 + BANDS] = np.cos(angle)
    table[1 + BANDS : FEATURES] = np.sin(angle)
    table[FEATURES] = 1.0
    return table


def dot(a, b, a_dim=1, b_dim=0, precision=EXACT):
    return lax.dot_general(
        a, b, (((a_dim,), (b_dim,)), ((), ())), precision=precision, preferred_element_type=F32
    )


def halves(v):
    high = v.astype(BF16)
    return high, (v - high.astype(F32)).astype(BF16)


def dot3(a, b, a_dim=1, b_dim=0):
    a_high, a_low = a
    b_high, b_low = b
    return (
        dot(a_high, b_high, a_dim, b_dim, None)
        + dot(a_high, b_low, a_dim, b_dim, None)
        + dot(a_low, b_high, a_dim, b_dim, None)
    )


def sin_cos(a):
    turns = jnp.floor(a * (2.0 / math.pi) + 0.5)
    r = a - turns * 1.5703125
    r = r - turns * 4.837512969970703125e-4
    r = r - turns * 7.549789954891882e-8
    r2 = r * r
    s = r + r * r2 * (-1.6666654611e-1 + r2 * (8.3321608736e-3 + r2 * -1.9515295891e-4))
    c = 1.0 - 0.5 * r2 + r2 * r2 * (4.166664568298827e-2 + r2 * (-1.388731625493765e-3 + r2 * 2.443315711809948e-5))
    q = turns.astype(jnp.int32)
    odd = (q & 1) == 1
    sine = jnp.where(odd, c, s)
    cosine = jnp.where(odd, s, c)
    sine = jnp.where((q & 2) == 2, -sine, sine)
    cosine = jnp.where(((q + 1) & 2) == 2, -cosine, cosine)
    return sine, cosine


def column(row):
    n = row.shape[1]
    hit = lax.broadcasted_iota(jnp.int32, (n, n), 0) == lax.broadcasted_iota(jnp.int32, (n, n), 1)
    return jnp.sum(jnp.where(hit, row, 0.0), axis=1, keepdims=True)


def kernel(
    x_hbm, g_hbm, high_hbm, low_hbm, inv_high_hbm, inv_low_hbm, feat_hbm, ew_hbm, eb_hbm, ef_hbm, mw_hbm, mb_hbm, mf_hbm, hw_hbm, dr_hbm,
    head_out, done_out,
    x_in, g_in, high, low, inv_high, inv_low, feat, ew, eb, ef, mw, mb, mf, hw, dr, send, recv,
    spec_0, spec_1, spec_2, spec_3,
    first_pre, first_cos, first_act, second_pre, second_cos, second_act, shaped, envelope,
    head_all, head_turned, packed, chan_recv, chan_total, seq_recv, half,
    local_sem, a2a_send, a2a_recv, head_send, head_recv, sum_send, sum_got, all_send, all_got,
    swap_sem, out_sem, row_sem,
):
    spec = spec_0, spec_1, spec_2, spec_3
    s = lax.axis_index("seq")
    c = lax.axis_index("chan")
    z = s // SEQ_SIDE
    y = s % SEQ_SIDE

    loads = [
        pltpu.make_async_copy(src, dst, local_sem.at[i])
        for i, (src, dst) in enumerate([
            (x_hbm, x_in), (g_hbm, g_in), (feat_hbm, feat), (ew_hbm, ew), (eb_hbm, eb), (ef_hbm, ef), (mw_hbm, mw),
            (mb_hbm, mb), (mf_hbm, mf), (hw_hbm, hw), (dr_hbm, dr), (high_hbm, high), (low_hbm, low),
            (inv_high_hbm, inv_high), (inv_low_hbm, inv_low),
        ])
    ]
    for load in loads:
        load.start()

    def along_z(d):
        return (z + d) % SEQ_SIDE * SEQ_SIDE + y

    def along_y(d):
        return z * SEQ_SIDE + (y + d) % SEQ_SIDE

    barrier = pltpu.get_barrier_semaphore()
    for d in range(1, SEQ_SIDE):
        pl.semaphore_signal(barrier, inc=1, device_id=(along_z(d), c), device_id_type=MESH)
        pl.semaphore_signal(barrier, inc=1, device_id=(along_y(d), c), device_id_type=MESH)
    for d in range(1, CHAN):
        pl.semaphore_signal(barrier, inc=1, device_id=(s, (c + d) % CHAN), device_id_type=MESH)

    def a2a(k, peer):
        return pltpu.make_async_remote_copy(
            src_ref=send.at[peer], dst_ref=recv.at[k], send_sem=a2a_send.at[k], recv_sem=a2a_recv.at[k],
            device_id=(peer, c), device_id_type=MESH,
        )

    def target(k):
        return (z + OFFSETS[k][0]) % SEQ_SIDE * SEQ_SIDE + (y + OFFSETS[k][1]) % SEQ_SIDE

    def source(k):
        return (z - OFFSETS[k][0] + SEQ_SIDE) % SEQ_SIDE * SEQ_SIDE + (y - OFFSETS[k][1] + SEQ_SIDE) % SEQ_SIDE

    loads[0].wait()
    loads[1].wait()
    for t in range(SEQ_SIDE):
        lanes = slice(t * 128, t * 128 + 128)
        rows = slice(t * SEQ_SIDE, (t + 1) * SEQ_SIDE)
        send[rows, 0:OWN, :] = x_in[:, lanes].T.reshape(SEQ_SIDE, OWN, BLOCK)
        send[rows, OWN : 2 * OWN, :] = g_in[:, lanes].T.reshape(SEQ_SIDE, OWN, BLOCK)

    pl.semaphore_wait(barrier, 2 * (SEQ_SIDE - 1) + CHAN - 1)
    for d in range(1, SEQ_SIDE):
        pl.semaphore_signal(row_sem, inc=1, device_id=(along_z(d), c), device_id_type=MESH)
    for k in range(STRAIGHT):
        a2a(k, target(k)).start()
    pl.semaphore_wait(row_sem, SEQ_SIDE - 1)
    for k in range(STRAIGHT, SEQ - 1):
        a2a(k, target(k)).start()

    for load in loads[2:11]:
        load.wait()
    ef_col = column(ef[...])
    mf_col = column(mf[...])
    features = feat[...]
    pre = dot(ew[...], features[:FEATURES, :], 0, 0) + column(eb[...])
    act, slope = sin_cos(ef_col * pre)
    first_pre[...] = pre
    first_cos[...] = slope
    first_act[0, 0:HIDDEN, :], first_act[1, 0:HIDDEN, :] = halves(act)
    first_act[0, HIDDEN:, :] = jnp.ones((16, FILTER_LEN), BF16)
    first_act[1, HIDDEN:, :] = jnp.zeros((16, FILTER_LEN), BF16)
    pre = dot(mw[...], act, 0, 0) + column(mb[...])
    act, slope = sin_cos(mf_col * pre)
    second_pre[...] = pre
    second_cos[...] = slope
    second_act[0], second_act[1] = halves(act)
    pick = lax.broadcasted_iota(jnp.int32, (OWN, BLOCK), 1) == lax.broadcasted_iota(jnp.int32, (OWN, BLOCK), 0) + OWN * s
    rates = jnp.sum(jnp.where(pick, dr[...], 0.0), axis=1, keepdims=True)
    picked = jnp.where(pick, 1.0, 0.0).astype(F32)
    head_rows = dot(picked, hw[...], 1, 1)
    head_cols = halves(dot(hw[...], picked, 1, 1))
    shaped[...] = dot(head_rows, act) * features[0:1, :]
    envelope[...] = jnp.exp(-features[0:1, :] * rates)

    def transform(tile, blocks, owners):
        lanes = slice(tile * 256, tile * 256 + 256)
        got = jnp.dot(blocks, high[:, lanes], preferred_element_type=F32)
        got += jnp.dot(blocks, low[:, lanes], preferred_element_type=F32)
        for i, owner in enumerate(owners):
            spec[tile][owner, :, :] = got[i * 2 * OWN : (i + 1) * 2 * OWN, :]

    def multiply(tile):
        parts_re, parts_im = [[] for _ in range(PARTS)], [[] for _ in range(PARTS)]
        for row in range(0, OWN, 8):
            xs, total_re, total_im = [], [None] * 4, [None] * 4
            for b in range(SEQ):
                x_rows, g_rows = slice(row, row + 8), slice(OWN + row, OWN + row + 8)
                xs.append((spec[tile][b, x_rows, 0:128], spec[tile][b, x_rows, 128:256]))
                g_re, g_im = spec[tile][b, g_rows, 0:128], spec[tile][b, g_rows, 128:256]
                for m in range(min(b, PARTS) + 1):
                    x_re, x_im = xs[b - m]
                    add_re = x_re * g_re + x_im * g_im
                    add_im = x_re * g_im - x_im * g_re
                    total_re[m] = add_re if total_re[m] is None else total_re[m] + add_re
                    total_im[m] = add_im if total_im[m] is None else total_im[m] + add_im
            for p in range(PARTS):
                if tile < TILES // 2:
                    parts_re[p].append(total_re[p] + total_im[p + 1])
                    parts_im[p].append(total_im[p] - total_re[p + 1])
                else:
                    parts_re[p].append(total_re[p] - total_im[p + 1])
                    parts_im[p].append(total_im[p] + total_re[p + 1])
        join = lambda parts: jnp.concatenate([v for part in parts for v in part], axis=0)
        return jnp.concatenate([join(parts_re), join(parts_im)], axis=1)

    recv[SEQ - 1] = send[s]
    loads[11].wait()
    loads[12].wait()
    for group in range(len(GROUPS) - 1):
        slots = list(range(GROUPS[group], GROUPS[group + 1]))
        for k in slots:
            a2a(k, source(k)).wait_recv()
        blocks = recv[slots[0] : slots[-1] + 1].reshape(len(slots) * 2 * OWN, BLOCK)
        owners = [source(k) for k in slots]
        if group == 0:
            blocks = jnp.concatenate([blocks, recv[SEQ - 1]], axis=0)
            owners.append(s)

        if group < len(GROUPS) - 2:
            for tile in range(TILES):
                transform(tile, blocks, owners)
    loads[13].wait()
    loads[14].wait()

    total = None
    for tile in range(TILES):
        transform(tile, blocks, owners)
        weights_high, weights_low = halves(multiply(tile))
        weights = jnp.concatenate([weights_high, weights_low], axis=0)
        rows = slice(tile * 256, tile * 256 + 256)
        both = jnp.dot(weights, inv_high[rows, :], preferred_element_type=F32)
        share = both[: PARTS * OWN] + both[PARTS * OWN :]
        share += jnp.dot(weights_high, inv_low[rows, :], preferred_element_type=F32)
        total = share if total is None else total + share
    lags = jnp.concatenate([total[p * OWN : (p + 1) * OWN, :] for p in range(PARTS)], axis=1)

    out_delta = lags * envelope[...]
    delta_halves = halves(out_delta)
    second_acts = second_act[0], second_act[1]
    mine = pl.ds(pl.multiple_of(s * OWN, OWN), OWN)
    head_all[mine, 0:HIDDEN] = dot3(delta_halves, second_acts, 1, 1)
    rate_grad = -jnp.sum(out_delta * shaped[...], axis=1, keepdims=True)
    head_all[mine, HIDDEN:128] = jnp.broadcast_to(rate_grad, (OWN, 128 - HIDDEN))

    def head_copy(slot, peer):
        rows = pl.ds(pl.multiple_of(slot * OWN, OWN), OWN)
        return pltpu.make_async_remote_copy(
            src_ref=head_all.at[rows], dst_ref=head_all.at[rows], send_sem=head_send.at[peer], recv_sem=head_recv.at[slot],
            device_id=(peer, c), device_id_type=MESH,
        )

    for d in range(1, SEQ):
        head_copy(s, (s + d) % SEQ).start()

    second_grad = dot3(head_cols, delta_halves)
    second_slope = second_grad * second_cos[...]
    second_delta = halves(second_slope * mf_col)
    first_slope = dot3(halves(mw[...]), second_delta) * first_cos[...]
    first_delta = halves(first_slope * ef_col)
    mixer_grad = dot3((first_act[0], first_act[1]), second_delta, 1, 1)
    embed_grad = dot3(halves(features), first_delta, 1, 1)
    ones = jnp.ones((8, FILTER_LEN), BF16)
    first_high, first_low = halves(first_slope * first_pre[...])
    second_high, second_low = halves(second_slope * second_pre[...])
    first_freq = dot(ones, first_high, 1, 1, None) + dot(ones, first_low, 1, 1, None)
    second_freq = dot(ones, second_high, 1, 1, None) + dot(ones, second_low, 1, 1, None)
    packed[0, :, 0:HIDDEN] = mixer_grad[0:24, :]
    packed[0, 0:16, HIDDEN:128] = mixer_grad[24:40, :]
    packed[0, 16:24, HIDDEN:128] = embed_grad[16:24, :]
    packed[1, :, 0:HIDDEN] = mixer_grad[40:64, :]
    packed[1, 0:16, HIDDEN:128] = embed_grad[0:16, :]
    packed[1, 16:17, HIDDEN:128] = first_freq[0:1, :]
    packed[1, 17:18, HIDDEN:128] = mixer_grad[HIDDEN : HIDDEN + 1, :]
    packed[1, 18:19, HIDDEN:128] = second_freq[0:1, :]
    packed[1, 19:24, HIDDEN:128] = jnp.zeros((5, 128 - HIDDEN), F32)

    def everything(ref, count, sem):
        some = ref.at[pl.ds(0, count)]
        return pltpu.make_async_remote_copy(
            src_ref=some, dst_ref=some, send_sem=sem.at[0], recv_sem=sem.at[0], device_id=(s, c), device_id_type=MESH
        )

    core = c % 2
    for d in range(1, CHAN):
        peer = (c + d) % CHAN
        pltpu.make_async_remote_copy(
            src_ref=packed.at[peer % 2], dst_ref=chan_recv.at[c], send_sem=sum_send.at[0], recv_sem=sum_got.at[0],
            device_id=(s, peer), device_id_type=MESH,
        ).start()
    chan_recv[c] = packed[core]
    everything(chan_recv, CHAN - 1, sum_got).wait_recv()
    chan_total[...] = jnp.sum(chan_recv[...], axis=0)
    for k in range(SEQ - 1):
        pltpu.make_async_remote_copy(
            src_ref=chan_total, dst_ref=seq_recv.at[s], send_sem=all_send.at[0], recv_sem=all_got.at[0],
            device_id=(target(k), c), device_id_type=MESH,
        ).start()
    seq_recv[s] = chan_total[...]

    for d in range(1, SEQ):
        peer = (s + d) % SEQ
        head_copy(peer, peer).wait_recv()
    head_turned[...] = head_all[...].T
    head_write = pltpu.make_async_copy(head_turned.at[0 : HIDDEN + 8], head_out, out_sem.at[0])
    head_write.start()
    for d in range(1, SEQ):
        a2a(d - 1, target(d - 1)).wait_send()
        head_copy(s, (s + d) % SEQ).wait_send()
    everything(chan_recv, CHAN - 1, sum_send).wait_send()

    everything(seq_recv, SEQ - 1, all_got).wait_recv()
    half[...] = jnp.sum(seq_recv[...], axis=0)
    swap = pltpu.make_async_remote_copy(
        src_ref=half, dst_ref=done_out.at[core], send_sem=swap_sem.at[0], recv_sem=swap_sem.at[1],
        device_id=(s, c + 1 - 2 * core), device_id_type=MESH,
    )
    swap.start()
    half_write = pltpu.make_async_copy(half, done_out.at[core], out_sem.at[1])
    half_write.start()
    everything(seq_recv, SEQ - 1, all_send).wait_send()
    head_write.wait()
    half_write.wait()
    swap.wait()


def hand_over(head, done, ew_out, eb_out, ef_out, mw_out, mb_out, mf_out, hw_out, dr_out):
    mw_out[0:24, :] = done[0, :, 0:HIDDEN]
    mw_out[24:40, :] = done[0, 0:16, HIDDEN:128]
    mw_out[40:64, :] = done[1, :, 0:HIDDEN]
    ew_out[0:16, :] = done[1, 0:16, HIDDEN:128]
    ew_out[16:17, :] = done[0, 16:17, HIDDEN:128]
    eb_out[...] = done[0, 17:18, HIDDEN:128]
    ef_out[...] = done[1, 16:17, HIDDEN:128]
    mb_out[...] = done[1, 17:18, HIDDEN:128]
    mf_out[...] = done[1, 18:19, HIDDEN:128]
    hw_out[...] = head[0:HIDDEN, :]
    dr_out[...] = head[HIDDEN : HIDDEN + 1, :]


def shards(inputs, out_grad, ew, eb, ef, mw, mb, mf, hw, dr):
    high, low, inv_high, inv_low = transform_table()
    row = lambda v: v.reshape(1, -1)
    vmem = pl.BlockSpec(memory_space=pltpu.VMEM)
    anywhere = pl.BlockSpec(memory_space=pl.ANY)
    out = lambda *shape: jax.ShapeDtypeStruct(shape, F32)
    shapes = (
        out(FEATURES, HIDDEN), out(1, HIDDEN), out(1, HIDDEN), out(HIDDEN, HIDDEN), out(1, HIDDEN), out(1, HIDDEN),
        out(HIDDEN, BLOCK), out(1, BLOCK),
    )
    taps = lambda rows: pltpu.VMEM((rows, FILTER_LEN), F32)
    dma = lambda n: pltpu.SemaphoreType.DMA((n,))
    got = pl.pallas_call(
        kernel,
        out_shape=(out(HIDDEN + 8, BLOCK), out(2, 24, 128)),
        in_specs=[anywhere] * 15,
        out_specs=(anywhere,) * 2,
        scratch_shapes=[
            pltpu.VMEM((BLOCK, BLOCK), BF16), pltpu.VMEM((BLOCK, BLOCK), BF16),
            pltpu.VMEM((BLOCK, 2 * BLOCK), BF16), pltpu.VMEM((BLOCK, 2 * BLOCK), BF16),
            pltpu.VMEM((2 * BLOCK, BLOCK), BF16), pltpu.VMEM((2 * BLOCK, BLOCK), BF16),
            taps(FEATURE_ROWS), pltpu.VMEM((FEATURES, HIDDEN), F32), pltpu.VMEM((1, HIDDEN), F32), pltpu.VMEM((1, HIDDEN), F32),
            pltpu.VMEM((HIDDEN, HIDDEN), F32), pltpu.VMEM((1, HIDDEN), F32), pltpu.VMEM((1, HIDDEN), F32),
            pltpu.VMEM((HIDDEN, BLOCK), F32), pltpu.VMEM((1, BLOCK), F32),
            pltpu.VMEM((SEQ, 2 * OWN, BLOCK), BF16), pltpu.VMEM((SEQ, 2 * OWN, BLOCK), BF16),
            *[pltpu.VMEM((SEQ, 2 * OWN, 256), F32)] * TILES,
            taps(HIDDEN), taps(HIDDEN), pltpu.VMEM((2, HIDDEN + 16, FILTER_LEN), BF16),
            taps(HIDDEN), taps(HIDDEN), pltpu.VMEM((2, HIDDEN, FILTER_LEN), BF16), taps(OWN), taps(OWN),
            pltpu.VMEM((BLOCK, 128), F32), pltpu.VMEM((128, BLOCK), F32), pltpu.VMEM((2, 24, 128), F32),
            pltpu.VMEM((CHAN, 24, 128), F32), pltpu.VMEM((24, 128), F32), pltpu.VMEM((SEQ, 24, 128), F32),
            pltpu.VMEM((24, 128), F32),
            dma(15), dma(SEQ), dma(SEQ), dma(SEQ), dma(SEQ), dma(1), dma(1), dma(1), dma(1), dma(2), dma(2), pltpu.SemaphoreType.REGULAR,
        ],
        compiler_params=pltpu.CompilerParams(
            collective_id=0, has_side_effects=True, vmem_limit_bytes=VMEM_LIMIT
        ),
    )(
        inputs, out_grad, jnp.asarray(high), jnp.asarray(low), jnp.asarray(inv_high), jnp.asarray(inv_low), jnp.asarray(tap_table()),
        ew, row(eb), row(ef), mw, row(mb), row(mf), hw, row(dr),
    )
    got = pl.pallas_call(
        hand_over,
        out_shape=shapes,
        in_specs=[vmem] * 2,
        out_specs=(vmem,) * 8,
    )(*got)
    ew_g, eb_g, ef_g, mw_g, mb_g, mf_g, hw_g, dr_g = got
    flat = lambda v: v.reshape(-1)
    return ew_g, flat(eb_g), flat(ef_g), mw_g, flat(mb_g), flat(mf_g), hw_g, flat(dr_g)


def solution(mesh):
    return jax.shard_map(
        shards,
        mesh=mesh,
        in_specs=(
            P("seq", "chan"), P("seq", "chan"), P(), P(), P(), P(), P(), P(), P(None, "chan"), P("chan"),
        ),
        out_specs=(P(), P(), P(), P(), P(), P(), P(None, "chan"), P("chan")),
        check_vma=False,
    )
```

```python
import math

import jax
import jax.numpy as jnp
import numpy as np
from jax import lax
from jax.experimental import pallas as pl
from jax.experimental.pallas import tpu as pltpu
from jax.sharding import PartitionSpec as P

MESH = pl.DeviceIdType.MESH
EXACT = lax.Precision.HIGHEST
F32 = jnp.float32
BF16 = jnp.bfloat16

FILTER_LEN = 1536
BANDS = 8
FEATURES = 17
FEATURE_ROWS = 24
HIDDEN = 64
BLOCK = 512
SEQ = 16
CHAN = 8
OWN = 32
PARTS = 3
SEQ_SIDE = 4
TILES = 4
VMEM_LIMIT = 60 * 1024 * 1024


def transform_table():
    order = np.concatenate([np.arange(0, BLOCK, 2), np.arange(1, BLOCK, 2)])
    turns = (2 * order[None, :] + 1) * np.arange(BLOCK)[:, None] % (4 * BLOCK)
    angle = turns * (2.0 * math.pi / (4 * BLOCK))
    table = np.stack([np.cos(angle).reshape(BLOCK, TILES, 128), -np.sin(angle).reshape(BLOCK, TILES, 128)], axis=2)
    table = table.reshape(BLOCK, 2 * BLOCK)
    high = table.astype(BF16)
    low = (table - high.astype(np.float64)).astype(BF16)
    inverse = lambda t: np.ascontiguousarray((t.astype(np.float32) / BLOCK).astype(BF16).T)
    return high, low, inverse(high), inverse(low)


STRAIGHT = 6
OFFSETS = [(2, 0), (0, 2), (0, 1), (0, 3), (1, 0), (3, 0)]
OFFSETS += [(2, 2), (1, 2), (2, 1), (2, 3), (3, 2), (1, 1), (1, 3), (3, 1), (3, 3)]
GROUPS = (0, 6, 10, 13, 15)


def tap_table():
    taps = np.arange(FILTER_LEN)
    freqs = np.array([max(1, FILTER_LEN // 4 // 2 ** (BANDS - level)) for level in range(1, BANDS + 1)])
    angle = (freqs[:, None] * taps[None, :] % FILTER_LEN) * (2.0 * math.pi / FILTER_LEN)
    table = np.zeros((FEATURE_ROWS, FILTER_LEN), np.float32)
    table[0] = taps / FILTER_LEN
    table[1 : 1 + BANDS] = np.cos(angle)
    table[1 + BANDS : FEATURES] = np.sin(angle)
    table[FEATURES] = 1.0
    return table


def dot(a, b, a_dim=1, b_dim=0, precision=EXACT):
    return lax.dot_general(
        a, b, (((a_dim,), (b_dim,)), ((), ())), precision=precision, preferred_element_type=F32
    )


def halves(v):
    high = v.astype(BF16)
    return high, (v - high.astype(F32)).astype(BF16)


def dot3(a, b, a_dim=1, b_dim=0):
    a_high, a_low = a
    b_high, b_low = b
    return (
        dot(a_high, b_high, a_dim, b_dim, None)
        + dot(a_high, b_low, a_dim, b_dim, None)
        + dot(a_low, b_high, a_dim, b_dim, None)
    )


def sin_cos(a):
    turns = jnp.floor(a * (2.0 / math.pi) + 0.5)
    r = a - turns * 1.5703125
    r = r - turns * 4.837512969970703125e-4
    r = r - turns * 7.549789954891882e-8
    r2 = r * r
    s = r + r * r2 * (-1.6666654611e-1 + r2 * (8.3321608736e-3 + r2 * -1.9515295891e-4))
    c = 1.0 - 0.5 * r2 + r2 * r2 * (4.166664568298827e-2 + r2 * (-1.388731625493765e-3 + r2 * 2.443315711809948e-5))
    q = turns.astype(jnp.int32)
    odd = (q & 1) == 1
    sine = jnp.where(odd, c, s)
    cosine = jnp.where(odd, s, c)
    sine = jnp.where((q & 2) == 2, -sine, sine)
    cosine = jnp.where(((q + 1) & 2) == 2, -cosine, cosine)
    return sine, cosine


def column(row):
    n = row.shape[1]
    hit = lax.broadcasted_iota(jnp.int32, (n, n), 0) == lax.broadcasted_iota(jnp.int32, (n, n), 1)
    return jnp.sum(jnp.where(hit, row, 0.0), axis=1, keepdims=True)


def kernel(
    x_hbm, g_hbm, high_hbm, low_hbm, inv_high_hbm, inv_low_hbm, feat_hbm, ew_hbm, eb_hbm, ef_hbm, mw_hbm, mb_hbm, mf_hbm, hw_hbm, dr_hbm,
    head_out, done_out,
    x_in, g_in, high, low, inv_high, inv_low, feat, ew, eb, ef, mw, mb, mf, hw, dr, send, recv,
    spec_0, spec_1, spec_2, spec_3,
    first_pre, first_cos, first_act, second_pre, second_cos, second_act, shaped, envelope,
    head_all, head_turned, packed, chan_recv, chan_total, seq_recv, half,
    local_sem, a2a_send, a2a_recv, head_send, head_recv, sum_send, sum_got, all_send, all_got,
    swap_sem, out_sem, row_sem,
):
    spec = spec_0, spec_1, spec_2, spec_3
    s = lax.axis_index("seq")
    c = lax.axis_index("chan")
    z = s // SEQ_SIDE
    y = s % SEQ_SIDE

    loads = [
        pltpu.make_async_copy(src, dst, local_sem.at[i])
        for i, (src, dst) in enumerate([
            (x_hbm, x_in), (g_hbm, g_in), (feat_hbm, feat), (ew_hbm, ew), (eb_hbm, eb), (ef_hbm, ef), (mw_hbm, mw),
            (mb_hbm, mb), (mf_hbm, mf), (hw_hbm, hw), (dr_hbm, dr), (high_hbm, high), (low_hbm, low),
            (inv_high_hbm, inv_high), (inv_low_hbm, inv_low),
        ])
    ]
    for load in loads:
        load.start()

    def along_z(d):
        return (z + d) % SEQ_SIDE * SEQ_SIDE + y

    def along_y(d):
        return z * SEQ_SIDE + (y + d) % SEQ_SIDE

    barrier = pltpu.get_barrier_semaphore()
    for d in range(1, SEQ_SIDE):
        pl.semaphore_signal(barrier, inc=1, device_id=(along_z(d), c), device_id_type=MESH)
        pl.semaphore_signal(barrier, inc=1, device_id=(along_y(d), c), device_id_type=MESH)
    for d in range(1, CHAN):
        pl.semaphore_signal(barrier, inc=1, device_id=(s, (c + d) % CHAN), device_id_type=MESH)

    def a2a(k, peer):
        return pltpu.make_async_remote_copy(
            src_ref=send.at[peer], dst_ref=recv.at[k], send_sem=a2a_send.at[k], recv_sem=a2a_recv.at[k],
            device_id=(peer, c), device_id_type=MESH,
        )

    def target(k):
        return (z + OFFSETS[k][0]) % SEQ_SIDE * SEQ_SIDE + (y + OFFSETS[k][1]) % SEQ_SIDE

    def source(k):
        return (z - OFFSETS[k][0] + SEQ_SIDE) % SEQ_SIDE * SEQ_SIDE + (y - OFFSETS[k][1] + SEQ_SIDE) % SEQ_SIDE

    loads[0].wait()
    loads[1].wait()
    for t in range(SEQ_SIDE):
        lanes = slice(t * 128, t * 128 + 128)
        rows = slice(t * SEQ_SIDE, (t + 1) * SEQ_SIDE)
        send[rows, 0:OWN, :] = x_in[:, lanes].T.reshape(SEQ_SIDE, OWN, BLOCK)
        send[rows, OWN : 2 * OWN, :] = g_in[:, lanes].T.reshape(SEQ_SIDE, OWN, BLOCK)

    pl.semaphore_wait(barrier, 2 * (SEQ_SIDE - 1) + CHAN - 1)
    for d in range(1, SEQ_SIDE):
        pl.semaphore_signal(row_sem, inc=1, device_id=(along_z(d), c), device_id_type=MESH)
    for k in range(STRAIGHT):
        a2a(k, target(k)).start()
    pl.semaphore_wait(row_sem, SEQ_SIDE - 1)
    for k in range(STRAIGHT, SEQ - 1):
        a2a(k, target(k)).start()

    for load in loads[2:11]:
        load.wait()
    ef_col = column(ef[...])
    mf_col = column(mf[...])
    features = feat[...]
    pre = dot(ew[...], features[:FEATURES, :], 0, 0) + column(eb[...])
    act, slope = sin_cos(ef_col * pre)
    first_pre[...] = pre
    first_cos[...] = slope
    first_act[0, 0:HIDDEN, :], first_act[1, 0:HIDDEN, :] = halves(act)
    first_act[0, HIDDEN:, :] = jnp.ones((16, FILTER_LEN), BF16)
    first_act[1, HIDDEN:, :] = jnp.zeros((16, FILTER_LEN), BF16)
    pre = dot(mw[...], act, 0, 0) + column(mb[...])
    act, slope = sin_cos(mf_col * pre)
    second_pre[...] = pre
    second_cos[...] = slope
    second_act[0], second_act[1] = halves(act)
    pick = lax.broadcasted_iota(jnp.int32, (OWN, BLOCK), 1) == lax.broadcasted_iota(jnp.int32, (OWN, BLOCK), 0) + OWN * s
    rates = jnp.sum(jnp.where(pick, dr[...], 0.0), axis=1, keepdims=True)
    picked = jnp.where(pick, 1.0, 0.0).astype(F32)
    head_rows = dot(picked, hw[...], 1, 1)
    head_cols = halves(dot(hw[...], picked, 1, 1))
    shaped[...] = dot(head_rows, act) * features[0:1, :]
    envelope[...] = jnp.exp(-features[0:1, :] * rates)

    def transform(tile, blocks, owners):
        lanes = slice(tile * 256, tile * 256 + 256)
        table = jnp.concatenate([high[:, lanes], low[:, lanes]], axis=0)
        got = jnp.dot(jnp.concatenate([blocks, blocks], axis=1), table, preferred_element_type=F32)
        for i, owner in enumerate(owners):
            spec[tile][owner, :, :] = got[i * 2 * OWN : (i + 1) * 2 * OWN, :]

    def multiply(tile):
        parts_re, parts_im = [[] for _ in range(PARTS)], [[] for _ in range(PARTS)]
        for row in range(0, OWN, 8):
            xs, total_re, total_im = [], [None] * 4, [None] * 4
            for b in range(SEQ):
                x_rows, g_rows = slice(row, row + 8), slice(OWN + row, OWN + row + 8)
                xs.append((spec[tile][b, x_rows, 0:128], spec[tile][b, x_rows, 128:256]))
                g_re, g_im = spec[tile][b, g_rows, 0:128], spec[tile][b, g_rows, 128:256]
                for m in range(min(b, PARTS) + 1):
                    x_re, x_im = xs[b - m]
                    add_re = x_re * g_re + x_im * g_im
                    add_im = x_re * g_im - x_im * g_re
                    total_re[m] = add_re if total_re[m] is None else total_re[m] + add_re
                    total_im[m] = add_im if total_im[m] is None else total_im[m] + add_im
            for p in range(PARTS):
                if tile < TILES // 2:
                    parts_re[p].append(total_re[p] + total_im[p + 1])
                    parts_im[p].append(total_im[p] - total_re[p + 1])
                else:
                    parts_re[p].append(total_re[p] - total_im[p + 1])
                    parts_im[p].append(total_im[p] + total_re[p + 1])
        join = lambda parts: jnp.concatenate([v for part in parts for v in part], axis=0)
        return jnp.concatenate([join(parts_re), join(parts_im)], axis=1)

    recv[SEQ - 1] = send[s]
    loads[11].wait()
    loads[12].wait()
    for group in range(len(GROUPS) - 1):
        slots = list(range(GROUPS[group], GROUPS[group + 1]))
        for k in slots:
            a2a(k, source(k)).wait_recv()
        blocks = recv[slots[0] : slots[-1] + 1].reshape(len(slots) * 2 * OWN, BLOCK)
        owners = [source(k) for k in slots]
        if group == 0:
            blocks = jnp.concatenate([blocks, recv[SEQ - 1]], axis=0)
            owners.append(s)

        if group < len(GROUPS) - 2:
            for tile in range(TILES):
                transform(tile, blocks, owners)
    loads[13].wait()
    loads[14].wait()

    total = None
    for tile in range(TILES):
        transform(tile, blocks, owners)
        weights_high, weights_low = halves(multiply(tile))
        weights = jnp.concatenate([weights_high, weights_low], axis=0)
        rows = slice(tile * 256, tile * 256 + 256)
        both = jnp.dot(weights, inv_high[rows, :], preferred_element_type=F32)
        share = both[: PARTS * OWN] + both[PARTS * OWN :]
        share += jnp.dot(weights_high, inv_low[rows, :], preferred_element_type=F32)
        total = share if total is None else total + share
    lags = jnp.concatenate([total[p * OWN : (p + 1) * OWN, :] for p in range(PARTS)], axis=1)

    out_delta = lags * envelope[...]
    delta_halves = halves(out_delta)
    second_acts = second_act[0], second_act[1]
    mine = pl.ds(pl.multiple_of(s * OWN, OWN), OWN)
    head_all[mine, 0:HIDDEN] = dot3(delta_halves, second_acts, 1, 1)
    rate_grad = -jnp.sum(out_delta * shaped[...], axis=1, keepdims=True)
    head_all[mine, HIDDEN:128] = jnp.broadcast_to(rate_grad, (OWN, 128 - HIDDEN))

    def head_copy(slot, peer):
        rows = pl.ds(pl.multiple_of(slot * OWN, OWN), OWN)
        return pltpu.make_async_remote_copy(
            src_ref=head_all.at[rows], dst_ref=head_all.at[rows], send_sem=head_send.at[peer], recv_sem=head_recv.at[slot],
            device_id=(peer, c), device_id_type=MESH,
        )

    for d in range(1, SEQ):
        head_copy(s, (s + d) % SEQ).start()

    second_grad = dot3(head_cols, delta_halves)
    second_slope = second_grad * second_cos[...]
    second_delta = halves(second_slope * mf_col)
    first_slope = dot3(halves(mw[...]), second_delta) * first_cos[...]
    first_delta = halves(first_slope * ef_col)
    mixer_grad = dot3((first_act[0], first_act[1]), second_delta, 1, 1)
    embed_grad = dot3(halves(features), first_delta, 1, 1)
    ones = jnp.ones((8, FILTER_LEN), BF16)
    first_high, first_low = halves(first_slope * first_pre[...])
    second_high, second_low = halves(second_slope * second_pre[...])
    first_freq = dot(ones, first_high, 1, 1, None) + dot(ones, first_low, 1, 1, None)
    second_freq = dot(ones, second_high, 1, 1, None) + dot(ones, second_low, 1, 1, None)
    packed[0, :, 0:HIDDEN] = mixer_grad[0:24, :]
    packed[0, 0:16, HIDDEN:128] = mixer_grad[24:40, :]
    packed[0, 16:24, HIDDEN:128] = embed_grad[16:24, :]
    packed[1, :, 0:HIDDEN] = mixer_grad[40:64, :]
    packed[1, 0:16, HIDDEN:128] = embed_grad[0:16, :]
    packed[1, 16:17, HIDDEN:128] = first_freq[0:1, :]
    packed[1, 17:18, HIDDEN:128] = mixer_grad[HIDDEN : HIDDEN + 1, :]
    packed[1, 18:19, HIDDEN:128] = second_freq[0:1, :]
    packed[1, 19:24, HIDDEN:128] = jnp.zeros((5, 128 - HIDDEN), F32)

    def everything(ref, count, sem):
        some = ref.at[pl.ds(0, count)]
        return pltpu.make_async_remote_copy(
            src_ref=some, dst_ref=some, send_sem=sem.at[0], recv_sem=sem.at[0], device_id=(s, c), device_id_type=MESH
        )

    core = c % 2
    for dx, swapped in ((2, 1), (1, 1), (3, 1), (2, 0), (1, 0), (3, 0), (0, 1)):
        peer = (c // 2 + dx) % (CHAN // 2) * 2 + (core + swapped) % 2
        pltpu.make_async_remote_copy(
            src_ref=packed.at[peer % 2], dst_ref=chan_recv.at[c], send_sem=sum_send.at[0], recv_sem=sum_got.at[0],
            device_id=(s, peer), device_id_type=MESH,
        ).start()
    chan_recv[c] = packed[core]
    everything(chan_recv, CHAN - 1, sum_got).wait_recv()
    chan_total[...] = jnp.sum(chan_recv[...], axis=0)
    for k in [*range(STRAIGHT, SEQ - 1), *range(STRAIGHT)]:
        pltpu.make_async_remote_copy(
            src_ref=chan_total, dst_ref=seq_recv.at[s], send_sem=all_send.at[0], recv_sem=all_got.at[0],
            device_id=(target(k), c), device_id_type=MESH,
        ).start()
    seq_recv[s] = chan_total[...]

    for d in range(1, SEQ):
        peer = (s + d) % SEQ
        head_copy(peer, peer).wait_recv()
    head_turned[...] = head_all[...].T
    head_write = pltpu.make_async_copy(head_turned.at[0 : HIDDEN + 8], head_out, out_sem.at[0])
    head_write.start()
    for d in range(1, SEQ):
        a2a(d - 1, target(d - 1)).wait_send()
        head_copy(s, (s + d) % SEQ).wait_send()
    everything(chan_recv, CHAN - 1, sum_send).wait_send()

    everything(seq_recv, SEQ - 1, all_got).wait_recv()
    half[...] = jnp.sum(seq_recv[...], axis=0)
    swap = pltpu.make_async_remote_copy(
        src_ref=half, dst_ref=done_out.at[core], send_sem=swap_sem.at[0], recv_sem=swap_sem.at[1],
        device_id=(s, c + 1 - 2 * core), device_id_type=MESH,
    )
    swap.start()
    half_write = pltpu.make_async_copy(half, done_out.at[core], out_sem.at[1])
    half_write.start()
    everything(seq_recv, SEQ - 1, all_send).wait_send()
    head_write.wait()
    half_write.wait()
    swap.wait()


def hand_over(head, done, ew_out, eb_out, ef_out, mw_out, mb_out, mf_out, hw_out, dr_out):
    mw_out[0:24, :] = done[0, :, 0:HIDDEN]
    mw_out[24:40, :] = done[0, 0:16, HIDDEN:128]
    mw_out[40:64, :] = done[1, :, 0:HIDDEN]
    ew_out[0:16, :] = done[1, 0:16, HIDDEN:128]
    ew_out[16:17, :] = done[0, 16:17, HIDDEN:128]
    eb_out[...] = done[0, 17:18, HIDDEN:128]
    ef_out[...] = done[1, 16:17, HIDDEN:128]
    mb_out[...] = done[1, 17:18, HIDDEN:128]
    mf_out[...] = done[1, 18:19, HIDDEN:128]
    hw_out[...] = head[0:HIDDEN, :]
    dr_out[...] = head[HIDDEN : HIDDEN + 1, :]


def shards(inputs, out_grad, ew, eb, ef, mw, mb, mf, hw, dr):
    high, low, inv_high, inv_low = transform_table()
    row = lambda v: v.reshape(1, -1)
    vmem = pl.BlockSpec(memory_space=pltpu.VMEM)
    anywhere = pl.BlockSpec(memory_space=pl.ANY)
    out = lambda *shape: jax.ShapeDtypeStruct(shape, F32)
    shapes = (
        out(FEATURES, HIDDEN), out(1, HIDDEN), out(1, HIDDEN), out(HIDDEN, HIDDEN), out(1, HIDDEN), out(1, HIDDEN),
        out(HIDDEN, BLOCK), out(1, BLOCK),
    )
    taps = lambda rows: pltpu.VMEM((rows, FILTER_LEN), F32)
    dma = lambda n: pltpu.SemaphoreType.DMA((n,))
    got = pl.pallas_call(
        kernel,
        out_shape=(out(HIDDEN + 8, BLOCK), out(2, 24, 128)),
        in_specs=[anywhere] * 15,
        out_specs=(anywhere,) * 2,
        scratch_shapes=[
            pltpu.VMEM((BLOCK, BLOCK), BF16), pltpu.VMEM((BLOCK, BLOCK), BF16),
            pltpu.VMEM((BLOCK, 2 * BLOCK), BF16), pltpu.VMEM((BLOCK, 2 * BLOCK), BF16),
            pltpu.VMEM((2 * BLOCK, BLOCK), BF16), pltpu.VMEM((2 * BLOCK, BLOCK), BF16),
            taps(FEATURE_ROWS), pltpu.VMEM((FEATURES, HIDDEN), F32), pltpu.VMEM((1, HIDDEN), F32), pltpu.VMEM((1, HIDDEN), F32),
            pltpu.VMEM((HIDDEN, HIDDEN), F32), pltpu.VMEM((1, HIDDEN), F32), pltpu.VMEM((1, HIDDEN), F32),
            pltpu.VMEM((HIDDEN, BLOCK), F32), pltpu.VMEM((1, BLOCK), F32),
            pltpu.VMEM((SEQ, 2 * OWN, BLOCK), BF16), pltpu.VMEM((SEQ, 2 * OWN, BLOCK), BF16),
            *[pltpu.VMEM((SEQ, 2 * OWN, 256), F32)] * TILES,
            taps(HIDDEN), taps(HIDDEN), pltpu.VMEM((2, HIDDEN + 16, FILTER_LEN), BF16),
            taps(HIDDEN), taps(HIDDEN), pltpu.VMEM((2, HIDDEN, FILTER_LEN), BF16), taps(OWN), taps(OWN),
            pltpu.VMEM((BLOCK, 128), F32), pltpu.VMEM((128, BLOCK), F32), pltpu.VMEM((2, 24, 128), F32),
            pltpu.VMEM((CHAN, 24, 128), F32), pltpu.VMEM((24, 128), F32), pltpu.VMEM((SEQ, 24, 128), F32),
            pltpu.VMEM((24, 128), F32),
            dma(15), dma(SEQ), dma(SEQ), dma(SEQ), dma(SEQ), dma(1), dma(1), dma(1), dma(1), dma(2), dma(2), pltpu.SemaphoreType.REGULAR,
        ],
        compiler_params=pltpu.CompilerParams(
            collective_id=0, has_side_effects=True, vmem_limit_bytes=VMEM_LIMIT
        ),
    )(
        inputs, out_grad, jnp.asarray(high), jnp.asarray(low), jnp.asarray(inv_high), jnp.asarray(inv_low), jnp.asarray(tap_table()),
        ew, row(eb), row(ef), mw, row(mb), row(mf), hw, row(dr),
    )
    got = pl.pallas_call(
        hand_over,
        out_shape=shapes,
        in_specs=[vmem] * 2,
        out_specs=(vmem,) * 8,
    )(*got)
    ew_g, eb_g, ef_g, mw_g, mb_g, mf_g, hw_g, dr_g = got
    flat = lambda v: v.reshape(-1)
    return ew_g, flat(eb_g), flat(ef_g), mw_g, flat(mb_g), flat(mf_g), hw_g, flat(dr_g)


def solution(mesh):
    return jax.shard_map(
        shards,
        mesh=mesh,
        in_specs=(
            P("seq", "chan"), P("seq", "chan"), P(), P(), P(), P(), P(), P(), P(None, "chan"), P("chan"),
        ),
        out_specs=(P(), P(), P(), P(), P(), P(), P(None, "chan"), P("chan")),
        check_vma=False,
    )
```

```python
import math

import jax
import jax.numpy as jnp
import numpy as np
from jax import lax
from jax.experimental import pallas as pl
from jax.experimental.pallas import tpu as pltpu
from jax.sharding import PartitionSpec as P

MESH = pl.DeviceIdType.MESH
EXACT = lax.Precision.HIGHEST
F32 = jnp.float32
BF16 = jnp.bfloat16

FILTER_LEN = 1536
BANDS = 8
FEATURES = 17
FEATURE_ROWS = 24
HIDDEN = 64
BLOCK = 512
SEQ = 16
CHAN = 8
OWN = 32
PARTS = 3
SEQ_SIDE = 4
TILES = 4
VMEM_LIMIT = 60 * 1024 * 1024


def transform_table():
    order = np.concatenate([np.arange(0, BLOCK, 2), np.arange(1, BLOCK, 2)])
    turns = (2 * order[None, :] + 1) * np.arange(BLOCK)[:, None] % (4 * BLOCK)
    angle = turns * (2.0 * math.pi / (4 * BLOCK))
    table = np.stack([np.cos(angle).reshape(BLOCK, TILES, 128), -np.sin(angle).reshape(BLOCK, TILES, 128)], axis=2)
    table = table.reshape(BLOCK, 2 * BLOCK)
    high = table.astype(BF16)
    low = (table - high.astype(np.float64)).astype(BF16)
    inverse = lambda t: np.ascontiguousarray((t.astype(np.float32) / BLOCK).astype(BF16).T)
    return high, low, inverse(high), inverse(low)


STRAIGHT = 6
OFFSETS = [(2, 0), (0, 2), (0, 1), (0, 3), (1, 0), (3, 0)]
OFFSETS += [(2, 2), (1, 2), (2, 1), (2, 3), (3, 2), (1, 1), (1, 3), (3, 1), (3, 3)]
GROUPS = (0, 6, 10, 13, 15)


def tap_table():
    taps = np.arange(FILTER_LEN)
    freqs = np.array([max(1, FILTER_LEN // 4 // 2 ** (BANDS - level)) for level in range(1, BANDS + 1)])
    angle = (freqs[:, None] * taps[None, :] % FILTER_LEN) * (2.0 * math.pi / FILTER_LEN)
    table = np.zeros((FEATURE_ROWS, FILTER_LEN), np.float32)
    table[0] = taps / FILTER_LEN
    table[1 : 1 + BANDS] = np.cos(angle)
    table[1 + BANDS : FEATURES] = np.sin(angle)
    table[FEATURES] = 1.0
    return table


def dot(a, b, a_dim=1, b_dim=0, precision=EXACT):
    return lax.dot_general(
        a, b, (((a_dim,), (b_dim,)), ((), ())), precision=precision, preferred_element_type=F32
    )


def halves(v):
    high = v.astype(BF16)
    return high, (v - high.astype(F32)).astype(BF16)


def dot3(a, b, a_dim=1, b_dim=0):
    a_high, a_low = a
    b_high, b_low = b
    return (
        dot(a_high, b_high, a_dim, b_dim, None)
        + dot(a_high, b_low, a_dim, b_dim, None)
        + dot(a_low, b_high, a_dim, b_dim, None)
    )


def sin_cos(a):
    turns = jnp.floor(a * (2.0 / math.pi) + 0.5)
    r = a - turns * 1.5703125
    r = r - turns * 4.837512969970703125e-4
    r = r - turns * 7.549789954891882e-8
    r2 = r * r
    s = r + r * r2 * (-1.6666654611e-1 + r2 * (8.3321608736e-3 + r2 * -1.9515295891e-4))
    c = 1.0 - 0.5 * r2 + r2 * r2 * (4.166664568298827e-2 + r2 * (-1.388731625493765e-3 + r2 * 2.443315711809948e-5))
    q = turns.astype(jnp.int32)
    odd = (q & 1) == 1
    sine = jnp.where(odd, c, s)
    cosine = jnp.where(odd, s, c)
    sine = jnp.where((q & 2) == 2, -sine, sine)
    cosine = jnp.where(((q + 1) & 2) == 2, -cosine, cosine)
    return sine, cosine


def column(row):
    n = row.shape[1]
    hit = lax.broadcasted_iota(jnp.int32, (n, n), 0) == lax.broadcasted_iota(jnp.int32, (n, n), 1)
    return jnp.sum(jnp.where(hit, row, 0.0), axis=1, keepdims=True)


def kernel(
    x_hbm, g_hbm, high_hbm, low_hbm, inv_high_hbm, inv_low_hbm, feat_hbm, ew_hbm, eb_hbm, ef_hbm, mw_hbm, mb_hbm, mf_hbm, hw_hbm, dr_hbm,
    head_out, done_out,
    x_in, g_in, high, low, inv_high, inv_low, feat, ew, eb, ef, mw, mb, mf, hw, dr, send, recv,
    spec_0, spec_1, spec_2, spec_3,
    first_pre, first_cos, first_act, second_pre, second_cos, second_act, shaped, envelope,
    head_all, head_turned, packed, chan_recv, chan_total, seq_recv, half,
    local_sem, a2a_send, a2a_recv, head_send, head_recv, sum_send, sum_got, all_send, all_got,
    swap_sem, out_sem, row_sem,
):
    spec = spec_0, spec_1, spec_2, spec_3
    s = lax.axis_index("seq")
    c = lax.axis_index("chan")
    z = s // SEQ_SIDE
    y = s % SEQ_SIDE

    loads = [
        pltpu.make_async_copy(src, dst, local_sem.at[i])
        for i, (src, dst) in enumerate([
            (x_hbm, x_in), (g_hbm, g_in), (feat_hbm, feat), (ew_hbm, ew), (eb_hbm, eb), (ef_hbm, ef), (mw_hbm, mw),
            (mb_hbm, mb), (mf_hbm, mf), (hw_hbm, hw), (dr_hbm, dr), (high_hbm, high), (low_hbm, low),
            (inv_high_hbm, inv_high), (inv_low_hbm, inv_low),
        ])
    ]
    def along_z(d):
        return (z + d) % SEQ_SIDE * SEQ_SIDE + y

    def along_y(d):
        return z * SEQ_SIDE + (y + d) % SEQ_SIDE

    barrier = pltpu.get_barrier_semaphore()
    for d in range(1, SEQ_SIDE):
        pl.semaphore_signal(barrier, inc=1, device_id=(along_z(d), c), device_id_type=MESH)
        pl.semaphore_signal(barrier, inc=1, device_id=(along_y(d), c), device_id_type=MESH)
    for d in range(1, CHAN):
        pl.semaphore_signal(barrier, inc=1, device_id=(s, (c + d) % CHAN), device_id_type=MESH)

    for load in loads:
        load.start()

    def a2a(k, peer):
        return pltpu.make_async_remote_copy(
            src_ref=send.at[peer], dst_ref=recv.at[k], send_sem=a2a_send.at[k], recv_sem=a2a_recv.at[k],
            device_id=(peer, c), device_id_type=MESH,
        )

    def target(k):
        return (z + OFFSETS[k][0]) % SEQ_SIDE * SEQ_SIDE + (y + OFFSETS[k][1]) % SEQ_SIDE

    def source(k):
        return (z - OFFSETS[k][0] + SEQ_SIDE) % SEQ_SIDE * SEQ_SIDE + (y - OFFSETS[k][1] + SEQ_SIDE) % SEQ_SIDE

    loads[0].wait()
    loads[1].wait()
    for t in range(SEQ_SIDE):
        lanes = slice(t * 128, t * 128 + 128)
        rows = slice(t * SEQ_SIDE, (t + 1) * SEQ_SIDE)
        send[rows, 0:OWN, :] = x_in[:, lanes].T.reshape(SEQ_SIDE, OWN, BLOCK)
        send[rows, OWN : 2 * OWN, :] = g_in[:, lanes].T.reshape(SEQ_SIDE, OWN, BLOCK)

    pl.semaphore_wait(barrier, 2 * (SEQ_SIDE - 1) + CHAN - 1)
    for d in range(1, SEQ_SIDE):
        pl.semaphore_signal(row_sem, inc=1, device_id=(along_z(d), c), device_id_type=MESH)
    for k in range(STRAIGHT):
        a2a(k, target(k)).start()
    pl.semaphore_wait(row_sem, SEQ_SIDE - 1)
    for k in range(STRAIGHT, SEQ - 1):
        a2a(k, target(k)).start()

    for load in loads[2:11]:
        load.wait()
    ef_col = column(ef[...])
    mf_col = column(mf[...])
    features = feat[...]
    pre = dot(ew[...], features[:FEATURES, :], 0, 0) + column(eb[...])
    act, slope = sin_cos(ef_col * pre)
    first_pre[...] = pre
    first_cos[...] = slope
    first_act[0, 0:HIDDEN, :], first_act[1, 0:HIDDEN, :] = halves(act)
    first_act[0, HIDDEN:, :] = jnp.ones((16, FILTER_LEN), BF16)
    first_act[1, HIDDEN:, :] = jnp.zeros((16, FILTER_LEN), BF16)
    pre = dot(mw[...], act, 0, 0) + column(mb[...])
    act, slope = sin_cos(mf_col * pre)
    second_pre[...] = pre
    second_cos[...] = slope
    second_act[0], second_act[1] = halves(act)
    pick = lax.broadcasted_iota(jnp.int32, (OWN, BLOCK), 1) == lax.broadcasted_iota(jnp.int32, (OWN, BLOCK), 0) + OWN * s
    rates = jnp.sum(jnp.where(pick, dr[...], 0.0), axis=1, keepdims=True)
    picked = jnp.where(pick, 1.0, 0.0).astype(F32)
    head_rows = dot(picked, hw[...], 1, 1)
    head_cols = halves(dot(hw[...], picked, 1, 1))
    shaped[...] = dot(head_rows, act) * features[0:1, :]
    envelope[...] = jnp.exp(-features[0:1, :] * rates)

    def transform(tile, blocks, owners):
        lanes = slice(tile * 256, tile * 256 + 256)
        table = jnp.concatenate([high[:, lanes], low[:, lanes]], axis=0)
        got = jnp.dot(jnp.concatenate([blocks, blocks], axis=1), table, preferred_element_type=F32)
        for i, owner in enumerate(owners):
            spec[tile][owner, :, :] = got[i * 2 * OWN : (i + 1) * 2 * OWN, :]

    def multiply(tile):
        parts_re, parts_im = [[] for _ in range(PARTS)], [[] for _ in range(PARTS)]
        for row in range(0, OWN, 8):
            xs, total_re, total_im = [], [None] * 4, [None] * 4
            for b in range(SEQ):
                x_rows, g_rows = slice(row, row + 8), slice(OWN + row, OWN + row + 8)
                xs.append((spec[tile][b, x_rows, 0:128], spec[tile][b, x_rows, 128:256]))
                g_re, g_im = spec[tile][b, g_rows, 0:128], spec[tile][b, g_rows, 128:256]
                for m in range(min(b, PARTS) + 1):
                    x_re, x_im = xs[b - m]
                    add_re = x_re * g_re + x_im * g_im
                    add_im = x_re * g_im - x_im * g_re
                    total_re[m] = add_re if total_re[m] is None else total_re[m] + add_re
                    total_im[m] = add_im if total_im[m] is None else total_im[m] + add_im
            for p in range(PARTS):
                if tile < TILES // 2:
                    parts_re[p].append(total_re[p] + total_im[p + 1])
                    parts_im[p].append(total_im[p] - total_re[p + 1])
                else:
                    parts_re[p].append(total_re[p] - total_im[p + 1])
                    parts_im[p].append(total_im[p] + total_re[p + 1])
        join = lambda parts: jnp.concatenate([v for part in parts for v in part], axis=0)
        return jnp.concatenate([join(parts_re), join(parts_im)], axis=1)

    recv[SEQ - 1] = send[s]
    loads[11].wait()
    loads[12].wait()
    for group in range(len(GROUPS) - 1):
        slots = list(range(GROUPS[group], GROUPS[group + 1]))
        for k in slots:
            a2a(k, source(k)).wait_recv()
        blocks = recv[slots[0] : slots[-1] + 1].reshape(len(slots) * 2 * OWN, BLOCK)
        owners = [source(k) for k in slots]
        if group == 0:
            blocks = jnp.concatenate([blocks, recv[SEQ - 1]], axis=0)
            owners.append(s)

        if group < len(GROUPS) - 2:
            for tile in range(TILES):
                transform(tile, blocks, owners)
    loads[13].wait()
    loads[14].wait()

    total = None
    for tile in range(TILES):
        transform(tile, blocks, owners)
        weights_high, weights_low = halves(multiply(tile))
        weights = jnp.concatenate([weights_high, weights_low], axis=0)
        rows = slice(tile * 256, tile * 256 + 256)
        both = jnp.dot(weights, inv_high[rows, :], preferred_element_type=F32)
        share = both[: PARTS * OWN] + both[PARTS * OWN :]
        share += jnp.dot(weights_high, inv_low[rows, :], preferred_element_type=F32)
        total = share if total is None else total + share
    lags = jnp.concatenate([total[p * OWN : (p + 1) * OWN, :] for p in range(PARTS)], axis=1)

    out_delta = lags * envelope[...]
    delta_halves = halves(out_delta)
    second_acts = second_act[0], second_act[1]
    mine = pl.ds(pl.multiple_of(s * OWN, OWN), OWN)
    head_all[mine, 0:HIDDEN] = dot3(delta_halves, second_acts, 1, 1)
    rate_grad = -jnp.sum(out_delta * shaped[...], axis=1, keepdims=True)
    head_all[mine, HIDDEN:128] = jnp.broadcast_to(rate_grad, (OWN, 128 - HIDDEN))

    def head_copy(slot, peer):
        rows = pl.ds(pl.multiple_of(slot * OWN, OWN), OWN)
        return pltpu.make_async_remote_copy(
            src_ref=head_all.at[rows], dst_ref=head_all.at[rows], send_sem=head_send.at[peer], recv_sem=head_recv.at[slot],
            device_id=(peer, c), device_id_type=MESH,
        )

    for d in range(1, SEQ):
        head_copy(s, (s + d) % SEQ).start()

    second_grad = dot3(head_cols, delta_halves)
    second_slope = second_grad * second_cos[...]
    second_delta = halves(second_slope * mf_col)
    first_slope = dot3(halves(mw[...]), second_delta) * first_cos[...]
    first_delta = halves(first_slope * ef_col)
    mixer_grad = dot3((first_act[0], first_act[1]), second_delta, 1, 1)
    embed_grad = dot3(halves(features), first_delta, 1, 1)
    ones = jnp.ones((8, FILTER_LEN), BF16)
    first_high, first_low = halves(first_slope * first_pre[...])
    second_high, second_low = halves(second_slope * second_pre[...])
    first_freq = dot(ones, first_high, 1, 1, None) + dot(ones, first_low, 1, 1, None)
    second_freq = dot(ones, second_high, 1, 1, None) + dot(ones, second_low, 1, 1, None)
    packed[0, :, 0:HIDDEN] = mixer_grad[0:24, :]
    packed[0, 0:16, HIDDEN:128] = mixer_grad[24:40, :]
    packed[0, 16:24, HIDDEN:128] = embed_grad[16:24, :]
    packed[1, :, 0:HIDDEN] = mixer_grad[40:64, :]
    packed[1, 0:16, HIDDEN:128] = embed_grad[0:16, :]
    packed[1, 16:17, HIDDEN:128] = first_freq[0:1, :]
    packed[1, 17:18, HIDDEN:128] = mixer_grad[HIDDEN : HIDDEN + 1, :]
    packed[1, 18:19, HIDDEN:128] = second_freq[0:1, :]
    packed[1, 19:24, HIDDEN:128] = jnp.zeros((5, 128 - HIDDEN), F32)

    def everything(ref, count, sem):
        some = ref.at[pl.ds(0, count)]
        return pltpu.make_async_remote_copy(
            src_ref=some, dst_ref=some, send_sem=sem.at[0], recv_sem=sem.at[0], device_id=(s, c), device_id_type=MESH
        )

    core = c % 2
    for dx, swapped in ((2, 1), (1, 1), (3, 1), (2, 0), (1, 0), (3, 0), (0, 1)):
        peer = (c // 2 + dx) % (CHAN // 2) * 2 + (core + swapped) % 2
        pltpu.make_async_remote_copy(
            src_ref=packed.at[peer % 2], dst_ref=chan_recv.at[c], send_sem=sum_send.at[0], recv_sem=sum_got.at[0],
            device_id=(s, peer), device_id_type=MESH,
        ).start()
    chan_recv[c] = packed[core]
    everything(chan_recv, CHAN - 1, sum_got).wait_recv()
    chan_total[...] = jnp.sum(chan_recv[...], axis=0)
    for k in [*range(STRAIGHT, SEQ - 1), *range(STRAIGHT)]:
        pltpu.make_async_remote_copy(
            src_ref=chan_total, dst_ref=seq_recv.at[s], send_sem=all_send.at[0], recv_sem=all_got.at[0],
            device_id=(target(k), c), device_id_type=MESH,
        ).start()
    seq_recv[s] = chan_total[...]

    for d in range(1, SEQ):
        peer = (s + d) % SEQ
        head_copy(peer, peer).wait_recv()
    head_turned[...] = head_all[...].T
    head_write = pltpu.make_async_copy(head_turned.at[0 : HIDDEN + 8], head_out, out_sem.at[0])
    head_write.start()
    for d in range(1, SEQ):
        a2a(d - 1, target(d - 1)).wait_send()
        head_copy(s, (s + d) % SEQ).wait_send()
    everything(chan_recv, CHAN - 1, sum_send).wait_send()

    everything(seq_recv, SEQ - 1, all_got).wait_recv()
    half[...] = jnp.sum(seq_recv[...], axis=0)
    swap = pltpu.make_async_remote_copy(
        src_ref=half, dst_ref=done_out.at[core], send_sem=swap_sem.at[0], recv_sem=swap_sem.at[1],
        device_id=(s, c + 1 - 2 * core), device_id_type=MESH,
    )
    swap.start()
    half_write = pltpu.make_async_copy(half, done_out.at[core], out_sem.at[1])
    half_write.start()
    everything(seq_recv, SEQ - 1, all_send).wait_send()
    head_write.wait()
    half_write.wait()
    swap.wait()


def hand_over(head, done, ew_out, eb_out, ef_out, mw_out, mb_out, mf_out, hw_out, dr_out):
    mw_out[0:24, :] = done[0, :, 0:HIDDEN]
    mw_out[24:40, :] = done[0, 0:16, HIDDEN:128]
    mw_out[40:64, :] = done[1, :, 0:HIDDEN]
    ew_out[0:16, :] = done[1, 0:16, HIDDEN:128]
    ew_out[16:17, :] = done[0, 16:17, HIDDEN:128]
    eb_out[...] = done[0, 17:18, HIDDEN:128]
    ef_out[...] = done[1, 16:17, HIDDEN:128]
    mb_out[...] = done[1, 17:18, HIDDEN:128]
    mf_out[...] = done[1, 18:19, HIDDEN:128]
    hw_out[...] = head[0:HIDDEN, :]
    dr_out[...] = head[HIDDEN : HIDDEN + 1, :]


def shards(inputs, out_grad, ew, eb, ef, mw, mb, mf, hw, dr):
    high, low, inv_high, inv_low = transform_table()
    row = lambda v: v.reshape(1, -1)
    vmem = pl.BlockSpec(memory_space=pltpu.VMEM)
    anywhere = pl.BlockSpec(memory_space=pl.ANY)
    out = lambda *shape: jax.ShapeDtypeStruct(shape, F32)
    shapes = (
        out(FEATURES, HIDDEN), out(1, HIDDEN), out(1, HIDDEN), out(HIDDEN, HIDDEN), out(1, HIDDEN), out(1, HIDDEN),
        out(HIDDEN, BLOCK), out(1, BLOCK),
    )
    taps = lambda rows: pltpu.VMEM((rows, FILTER_LEN), F32)
    dma = lambda n: pltpu.SemaphoreType.DMA((n,))
    got = pl.pallas_call(
        kernel,
        out_shape=(out(HIDDEN + 8, BLOCK), out(2, 24, 128)),
        in_specs=[anywhere] * 15,
        out_specs=(anywhere,) * 2,
        scratch_shapes=[
            pltpu.VMEM((BLOCK, BLOCK), BF16), pltpu.VMEM((BLOCK, BLOCK), BF16),
            pltpu.VMEM((BLOCK, 2 * BLOCK), BF16), pltpu.VMEM((BLOCK, 2 * BLOCK), BF16),
            pltpu.VMEM((2 * BLOCK, BLOCK), BF16), pltpu.VMEM((2 * BLOCK, BLOCK), BF16),
            taps(FEATURE_ROWS), pltpu.VMEM((FEATURES, HIDDEN), F32), pltpu.VMEM((1, HIDDEN), F32), pltpu.VMEM((1, HIDDEN), F32),
            pltpu.VMEM((HIDDEN, HIDDEN), F32), pltpu.VMEM((1, HIDDEN), F32), pltpu.VMEM((1, HIDDEN), F32),
            pltpu.VMEM((HIDDEN, BLOCK), F32), pltpu.VMEM((1, BLOCK), F32),
            pltpu.VMEM((SEQ, 2 * OWN, BLOCK), BF16), pltpu.VMEM((SEQ, 2 * OWN, BLOCK), BF16),
            *[pltpu.VMEM((SEQ, 2 * OWN, 256), F32)] * TILES,
            taps(HIDDEN), taps(HIDDEN), pltpu.VMEM((2, HIDDEN + 16, FILTER_LEN), BF16),
            taps(HIDDEN), taps(HIDDEN), pltpu.VMEM((2, HIDDEN, FILTER_LEN), BF16), taps(OWN), taps(OWN),
            pltpu.VMEM((BLOCK, 128), F32), pltpu.VMEM((128, BLOCK), F32), pltpu.VMEM((2, 24, 128), F32),
            pltpu.VMEM((CHAN, 24, 128), F32), pltpu.VMEM((24, 128), F32), pltpu.VMEM((SEQ, 24, 128), F32),
            pltpu.VMEM((24, 128), F32),
            dma(15), dma(SEQ), dma(SEQ), dma(SEQ), dma(SEQ), dma(1), dma(1), dma(1), dma(1), dma(2), dma(2), pltpu.SemaphoreType.REGULAR,
        ],
        compiler_params=pltpu.CompilerParams(
            collective_id=0, has_side_effects=True, vmem_limit_bytes=VMEM_LIMIT
        ),
    )(
        inputs, out_grad, jnp.asarray(high), jnp.asarray(low), jnp.asarray(inv_high), jnp.asarray(inv_low), jnp.asarray(tap_table()),
        ew, row(eb), row(ef), mw, row(mb), row(mf), hw, row(dr),
    )
    got = pl.pallas_call(
        hand_over,
        out_shape=shapes,
        in_specs=[vmem] * 2,
        out_specs=(vmem,) * 8,
    )(*got)
    ew_g, eb_g, ef_g, mw_g, mb_g, mf_g, hw_g, dr_g = got
    flat = lambda v: v.reshape(-1)
    return ew_g, flat(eb_g), flat(ef_g), mw_g, flat(mb_g), flat(mf_g), hw_g, flat(dr_g)


def solution(mesh):
    return jax.shard_map(
        shards,
        mesh=mesh,
        in_specs=(
            P("seq", "chan"), P("seq", "chan"), P(), P(), P(), P(), P(), P(), P(None, "chan"), P("chan"),
        ),
        out_specs=(P(), P(), P(), P(), P(), P(), P(None, "chan"), P("chan")),
        check_vma=False,
    )
```
